256 devices in a mesh: lon: 16 (over y, x_hi, core), lat: 16 (over x_lo, z).
Axes of the slice: x: 4 (x_hi: 2, x_lo: 2; x = x_hi * 2 + x_lo), y: 4, z: 8, core: 2. Of those that a mesh axis runs over, the one named last changes fastest.
Arguments:
- inputs: bfloat16 [2, 96, 192, 512], P(None, 'lat', 'lon'), may hold values from -6 to 6
- cotangent: bfloat16 [2, 96, 192, 512], P(None, 'lat', 'lon'), may hold values from -6 to 6
- gains: float32 [2, 512], replicated, may hold values from 0.1 to 1.9
- w_qkv: bfloat16 [2, 512, 1536], replicated, may hold values from -2 to 2
- w_out: bfloat16 [2, 512, 512], replicated, may hold values from -0.25 to 0.25
Outputs:
- grad_inputs: bfloat16 [2, 96, 192, 512], P(None, 'lat', 'lon')
- grad_qkv: float32 [2, 512, 1536], P(None, 'lon')
- grad_out: float32 [2, 512, 512], P(None, 'lon')
- grad_gains: float32 [2, 512], replicated
The draws below stay inside these ranges and needn't reach their ends.
All inputs are finite; a program needn't handle non-finite values.
Results may differ from the reference program's by a relative error of at most 0.03.
Values may be sent and summed in bfloat16 or wider, within the bound.
A program may use at most 64 MiB of HBM per device.

```python
import jax
import jax.numpy as jnp
from jax import lax

D = 512
HEADS = 8
LEV = 2
WLAT = 6
WLON = 12
NLAT = 96
NLON = 192


def draw_w_qkv(key, part):
    key = jax.random.fold_in(key, 11)
    first = jax.random.fold_in(key, 0)
    deviation = D ** (-0.5)
    base = jnp.clip(jax.random.normal(first, (2, D, 3 * D), jnp.float32), -5.0, 5.0) * deviation
    return base.astype(jnp.bfloat16)


def shard_levels(stream_key, extent, shards, least, top_value):
    factor_of, own = 1.0, jax.random.fold_in(stream_key, 6)
    for dim, blocks in shards:
        heights = jnp.exp(jax.random.uniform(jax.random.fold_in(own, dim), (blocks,), jnp.float32, least / len(shards), top_value / len(shards)))
        factor_of = factor_of * jnp.repeat(heights, extent[dim] // blocks).reshape([-1 if axis == dim else 1 for axis in range(len(extent))])
    return factor_of


def gaussian(stream_key, dims, scale, reach, pieces=(), kind=jnp.bfloat16):
    array = jax.random.normal(stream_key, dims, jnp.float32) * scale
    if len(pieces) > 0:
        array = shard_levels(stream_key, dims, pieces, -0.22, 0.18) * array
    return jnp.clip(array, min=-reach, max=reach).astype(kind)


def setup_inputs(seed: int = 0) -> dict:
    key_of = jax.random.split(jax.random.key(seed), 6)
    return {
        "inputs": gaussian(key_of[0], (LEV, NLAT, NLON, D), 1.0, 6.0, ((1, 16), (2, 16))),
        "cotangent": gaussian(key_of[1], (LEV, NLAT, NLON, D), 1.0, 6.0, ((1, 16), (2, 16))),
        "gains": jnp.clip(1.0 + 0.18 * jax.random.normal(key_of[2], (2, D), jnp.float32), 0.1, 1.9),
        "w_qkv": draw_w_qkv(jax.random.fold_in(key_of[5], 71), 0),
        "w_out": gaussian(key_of[4], (2, D, D), D ** -0.5, 0.25),
    }


epsilon = 1e-05
masked = -1e+30

def to_windows(field_grid):
    levels, lat_rows, lon_cols, feature = field_grid.shape
    field_grid = field_grid.reshape(levels, lat_rows // WLAT, WLAT, lon_cols // WLON, WLON, feature)
    field_grid = field_grid.transpose(1, 3, 0, 2, 4, 5)
    return field_grid.reshape(lat_rows // WLAT, lon_cols // WLON, levels * WLAT * WLON, feature)

def from_windows(blocks):
    win_rows, win_cols, win_size, feature = blocks.shape
    blocks = blocks.reshape(win_rows, win_cols, LEV, WLAT, WLON, feature)
    blocks = blocks.transpose(2, 0, 3, 1, 4, 5)
    return blocks.reshape(LEV, win_rows * WLAT, win_cols * WLON, feature)

def region_windows(row_ids):
    per_row = row_ids.reshape(-1, WLAT)
    spread_ids = jnp.broadcast_to(per_row[:, None, :, None], (per_row.shape[0], LEV, WLAT, WLON))
    return spread_ids.reshape(per_row.shape[0], LEV * WLAT * WLON)

def window_scores(projected, region):
    win_cols, win_size, triple = projected.shape
    head_size = triple // (3 * HEADS)
    split_heads = projected.reshape(win_cols, win_size, 3, HEADS, head_size).astype(jnp.float32)
    queries = split_heads[:, :, 0]
    keys_all = split_heads[:, :, 1]
    values_all = split_heads[:, :, 2]
    scale = head_size ** (-0.5)
    scores = jnp.einsum('nihe,njhe->nhij', queries, keys_all) * scale
    same_region = region[:, None] == region[None, :]
    scores = jnp.where(same_region, scores, masked)
    row_max = lax.optimization_barrier(jnp.max(scores, axis=-1, keepdims=True))
    exponent = jnp.exp(scores - row_max)
    weights = exponent / lax.optimization_barrier(jnp.sum(exponent, axis=-1, keepdims=True))
    return (weights, queries, keys_all, values_all, scale)

def attend_forward(pair):
    projected, region = pair
    weights, queries, keys_all, values_all, scale = window_scores(projected, region)
    rounded = lax.optimization_barrier(weights.astype(jnp.bfloat16)).astype(jnp.float32)
    mixed = jnp.einsum('nhij,njhe->nihe', rounded, values_all)
    return mixed.reshape(projected.shape[0], projected.shape[1], -1).astype(jnp.bfloat16)

def attend_backward(triple_in):
    projected, region, grad_mixed = triple_in
    weights, queries, keys_all, values_all, scale = window_scores(projected, region)
    rounded = lax.optimization_barrier(weights.astype(jnp.bfloat16)).astype(jnp.float32)
    grad_heads = grad_mixed.reshape(queries.shape).astype(jnp.float32)
    grad_weights = jnp.einsum('nihe,njhe->nhij', grad_heads, values_all)
    grad_values = jnp.einsum('nhij,nihe->njhe', rounded, grad_heads).astype(jnp.bfloat16)
    grad_scores = weights * (grad_weights - lax.optimization_barrier(jnp.sum(grad_weights * weights, axis=-1, keepdims=True)))
    grad_scores = lax.optimization_barrier(grad_scores.astype(jnp.bfloat16)).astype(jnp.float32)
    grad_queries = (jnp.einsum('nhij,njhe->nihe', grad_scores, keys_all) * scale).astype(jnp.bfloat16)
    grad_keys = (jnp.einsum('nhij,nihe->njhe', grad_scores, queries) * scale).astype(jnp.bfloat16)
    stacked = jnp.stack([grad_queries, grad_keys, grad_values], axis=2)
    return stacked.reshape(projected.shape)

def layer_forward(blocks, gain_row, w_qkv, region):
    feature = blocks.shape[-1]
    values32 = blocks.astype(jnp.float32)
    center = lax.optimization_barrier(jnp.mean(values32, axis=-1, keepdims=True))
    spread = lax.optimization_barrier(jnp.mean(jnp.square(values32 - center), axis=-1, keepdims=True))
    inverse = lax.rsqrt(spread + epsilon)
    standard = (values32 - center) * inverse
    normed = (standard * gain_row).astype(jnp.bfloat16)
    projected = jnp.dot(normed.reshape(-1, feature), w_qkv, preferred_element_type=jnp.float32).astype(jnp.bfloat16)
    projected = projected.reshape(blocks.shape[:-1] + (3 * feature,))
    attended = lax.map(attend_forward, (projected, region))
    return (standard, inverse, normed, projected, attended)

def layer_output(blocks, attended, w_out):
    feature = blocks.shape[-1]
    branch = jnp.dot(attended.reshape(-1, feature), w_out, preferred_element_type=jnp.float32)
    return (blocks.astype(jnp.float32) + branch.reshape(blocks.shape)).astype(jnp.bfloat16)

def layer_backward(grad_y, saved, gain_row, w_qkv, w_out, region):
    standard, inverse, normed, projected, attended = saved
    feature = grad_y.shape[-1]
    grad_flat = grad_y.reshape(-1, feature)
    grad_wout = jnp.dot(attended.reshape(-1, feature).T, grad_flat, preferred_element_type=jnp.float32)
    grad_att = jnp.dot(grad_flat, w_out.T, preferred_element_type=jnp.float32).astype(jnp.bfloat16)
    grad_att = grad_att.reshape(attended.shape)
    grad_proj = lax.map(attend_backward, (projected, region, grad_att))
    proj_flat = grad_proj.reshape(-1, 3 * feature)
    grad_wqkv = jnp.dot(normed.reshape(-1, feature).T, proj_flat, preferred_element_type=jnp.float32)
    grad_normed = jnp.dot(proj_flat, w_qkv.T, preferred_element_type=jnp.float32).reshape(standard.shape)
    grad_gain = lax.optimization_barrier(jnp.sum(grad_normed * standard, axis=(0, 1, 2)))
    scaled = grad_normed * gain_row
    centered = scaled - lax.optimization_barrier(jnp.mean(scaled, axis=-1, keepdims=True))
    centered = centered - standard * lax.optimization_barrier(jnp.mean(scaled * standard, axis=-1, keepdims=True))
    grad_in = grad_y.astype(jnp.float32) + inverse * centered
    return (grad_in.astype(jnp.bfloat16), grad_wqkv, grad_wout, grad_gain)

def reference(inputs, cotangent, gains, w_qkv, w_out):
    half_lat = WLAT // 2
    half_lon = WLON // 2
    blocks = to_windows(inputs)
    plain_region = jnp.zeros((NLAT // WLAT, LEV * WLAT * WLON), jnp.int32)
    saved_first = layer_forward(blocks, gains[0], w_qkv[0], plain_region)
    middle = from_windows(layer_output(blocks, saved_first[4], w_out[0]))
    shifted = jnp.roll(middle, (-half_lat, -half_lon), axis=(1, 2))
    shifted_grad = jnp.roll(cotangent, (-half_lat, -half_lon), axis=(1, 2))
    row_ids = jnp.where(jnp.arange(NLAT) >= NLAT - half_lat, 1, 0).astype(jnp.int32)
    region = region_windows(row_ids)
    saved_second = layer_forward(to_windows(shifted), gains[1], w_qkv[1], region)
    grad_shifted, qkv_second, out_second, gain_second = layer_backward(to_windows(shifted_grad), saved_second, gains[1], w_qkv[1], w_out[1], region)
    grad_middle = jnp.roll(from_windows(grad_shifted), (half_lat, half_lon), axis=(1, 2))
    grad_blocks, qkv_first, out_first, gain_first = layer_backward(to_windows(grad_middle), saved_first, gains[0], w_qkv[0], w_out[0], plain_region)
    return (from_windows(grad_blocks), jnp.stack([qkv_first, qkv_second]), jnp.stack([out_first, out_second]), jnp.stack([gain_first, gain_second]))
```

```python
import functools

import jax
import jax.numpy as jnp
import numpy as np
from jax import lax
from jax.experimental import pallas as pl
from jax.experimental.pallas import tpu as pltpu
from jax.sharding import PartitionSpec as P

MESH = pl.DeviceIdType.MESH
F32 = jnp.float32
BF16 = jnp.bfloat16

HEADS = 8
LEV = 2
WLAT = 6
WLON = 12
D = 512
EPS = 1e-05
MASKED = -1e30
TOK = LEV * WLAT * WLON
QUAD = TOK // 4
PADQ = 48
STACK = 4 * TOK


def dot(a, b):
    return lax.dot_general(a, b, (((1,), (0,)), ((), ())), preferred_element_type=F32)


def dot_nt(a, b):
    return lax.dot_general(a, b, (((1,), (1,)), ((), ())), preferred_element_type=F32)


def dot_tn(a, b):
    return lax.dot_general(a, b, (((0,), (0,)), ((), ())), preferred_element_type=F32)


def slab_pieces():
    for lev in range(LEV):
        for row in range(WLAT):
            half_r, r = divmod(row, WLAT // 2)
            starts = [
                (half_r * 2 + half_c) * QUAD + lev * (QUAD // 2) + r * (WLON // 2)
                for half_c in range(2)
            ]
            yield lev, row, starts


def kernel(
    n_lat,
    n_lon,
    x_ref,
    c_ref,
    gains_ref,
    wq_ref,
    wo_ref,
    gx_ref,
    gq_ref,
    go_ref,
    gg_ref,
    xs,
    gy,
    std,
    inv,
    proj,
    qm,
    gam,
    probs,
    probs16,
    att,
    tmp,
    scores,
    ds,
    gp,
    gy16,
    na_own,
    na_out,
    na_in,
    gp_in,
    gy_in,
    hs,
    hr,
    gsend,
    r1a,
    r1b,
    acca,
    accb,
    r2a,
    r2b,
    acc2,
    r3,
    fin,
    gain_c,
    gain_y,
    gain_x,
    gain_z,
    send_sem,
    recv_sem,
):
    a = lax.axis_index("lat")
    b = lax.axis_index("lon")
    n_z = n_lat // 2
    n_y = n_lon // 4
    xlo, z = a // n_z, a % n_z
    y, xhi, core = b // 4, (b // 2) % 2, b % 2
    x = xhi * 2 + xlo

    def at(lat, lon):
        return {"lat": lat, "lon": lon}

    def at_x(xx):
        return at((xx % 2) * n_z + z, y * 4 + (xx // 2) * 2 + core)

    def at_y(yy):
        return at(a, yy * 4 + xhi * 2 + core)

    def at_z(zz):
        return at(xlo * n_z + zz, b)

    up_a, dn_a = (a + 1) % n_lat, (a + n_lat - 1) % n_lat
    up_b, dn_b = (b + 1) % n_lon, (b + n_lon - 1) % n_lon
    partner = at(a, y * 4 + xhi * 2 + (1 - core))
    halo_down = [at(dn_a, dn_b), at(dn_a, b), at(a, dn_b)]
    halo_up = [at(up_a, up_b), at(up_a, b), at(a, up_b)]

    greet = halo_down + halo_up + [partner]
    greet += [at_y((y + k) % n_y) for k in range(1, n_y)]
    greet += [at_x((x + k) % 4) for k in range(1, 4)]
    greet += [at((a + k) % n_lat, b) for k in range(1, n_lat)]
    barrier = pltpu.get_barrier_semaphore()
    for device in greet:
        pl.semaphore_signal(barrier, inc=1, device_id=device, device_id_type=MESH)

    count = [0]
    pending = []

    def remote(src, dst, device):
        i = count[0]
        count[0] += 1
        copy = pltpu.make_async_remote_copy(
            src_ref=src,
            dst_ref=dst,
            send_sem=send_sem.at[i],
            recv_sem=recv_sem.at[i],
            device_id=device,
            device_id_type=MESH,
        )
        copy.start()
        pending.append(copy)
        return copy

    def expect(i, src, dst, device):
        return pltpu.make_async_remote_copy(
            src_ref=src,
            dst_ref=dst,
            send_sem=send_sem.at[i],
            recv_sem=recv_sem.at[i],
            device_id=device,
            device_id_type=MESH,
        )

    lane = lax.broadcasted_iota(jnp.int32, (1, 256), 1)
    head_mask = [((lane >= 64 * h) & (lane < 64 * h + 64)).astype(F32) for h in range(4)]
    mask16 = [m.astype(BF16) for m in head_mask]
    scaled16 = [(m * 0.125).astype(BF16) for m in head_mask]

    r_id = lax.broadcasted_iota(jnp.int32, (D, D), 0)
    c_id = lax.broadcasted_iota(jnp.int32, (D, D), 1)
    low = c_id & 255
    which = jnp.where(c_id < 256, core, 1 - core)
    pick = (r_id == ((low >> 5) * 64 + which * 32 + (low & 31))).astype(F32).astype(BF16)

    def select_heads(stacked_ref):
        out = stacked_ref[0:TOK, :] * head_mask[0]
        for h in range(1, 4):
            out = jnp.where(head_mask[h] > 0.5, stacked_ref[h * TOK : (h + 1) * TOK, :], out)
        return out

    def forward(l):
        u = xs[l]
        center = jnp.mean(u, axis=-1, keepdims=True)
        u = u - center
        spread = jnp.mean(u * u, axis=-1, keepdims=True)
        inverse = lax.rsqrt(spread + EPS)
        standard = u * inverse
        std[l] = standard
        inv[l] = inverse
        normed = (standard * gains_ref[l : l + 1, :]).astype(BF16)
        proj[l] = dot(normed, wq_ref[l]).astype(BF16)
        both = dot(normed, pick).astype(BF16)
        na_own[l, 0] = both[:, :256]
        na_out[l, 0] = both[:, 256:]
        for t in range(2):
            q = proj[l, :, 256 * t : 256 * t + 256]
            k = proj[l, :, D + 256 * t : D + 256 * t + 256]
            v = proj[l, :, 2 * D + 256 * t : 2 * D + 256 * t + 256]
            for h in range(4):
                qm[l, t, h * TOK : (h + 1) * TOK, :] = q * scaled16[h]
            scores[...] = dot_nt(qm[l, t], k)
            for h in range(4):
                rows = slice(h * TOK, (h + 1) * TOK)
                s = scores[rows, :]
                if l == 1:
                    s = jnp.where(same_region, s, MASKED)
                e = jnp.exp(s - jnp.max(s, axis=-1, keepdims=True))
                p = e * (1.0 / jnp.sum(e, axis=-1, keepdims=True))
                probs[l, t, rows, :] = p
                probs16[l, t, rows, :] = p.astype(BF16)
            tmp[...] = dot(probs16[l, t], v)
            att[l, :, 256 * t : 256 * t + 256] = select_heads(tmp).astype(BF16)
        both = dot(att[l], pick).astype(BF16)
        na_own[l, 1] = both[:, :256]
        na_out[l, 1] = both[:, 256:]

    def backward_attention(l, t):
        k = proj[l, :, D + 256 * t : D + 256 * t + 256]
        v = proj[l, :, 2 * D + 256 * t : 2 * D + 256 * t + 256]
        g = dot_nt(gy16[l], wo_ref[l, 256 * t : 256 * t + 256, :]).astype(BF16)
        for h in range(4):
            gam[h * TOK : (h + 1) * TOK, :] = g * mask16[h]
        scores[...] = dot_nt(gam[...], v)
        gp[l, :, 2 * D + 256 * t : 2 * D + 256 * t + 256] = dot_tn(probs16[l, t], gam[...]).astype(BF16)
        for h in range(4):
            rows = slice(h * TOK, (h + 1) * TOK)
            p = probs[l, t, rows, :]
            g_p = scores[rows, :]
            total = jnp.sum(g_p * p, axis=-1, keepdims=True)
            ds[rows, :] = (p * (g_p - total)).astype(BF16)
        gp[l, :, D + 256 * t : D + 256 * t + 256] = dot_tn(ds[...], qm[l, t]).astype(BF16)
        tmp[...] = dot(ds[...], k)
        gp[l, :, 256 * t : 256 * t + 256] = (select_heads(tmp) * 0.125).astype(BF16)

    def backward_input(l):
        grad_normed = dot_nt(gp[l], wq_ref[l])
        standard = std[l]
        gain_rows = jnp.sum(grad_normed * standard, axis=0, keepdims=True)
        for j in range(4):
            gain_c[pl.ds(core, 1), l * 4 + j : l * 4 + j + 1, :] = gain_rows[
                :, j * 128 : (j + 1) * 128
            ].reshape(1, 1, 128)
        scaled = grad_normed * gains_ref[l : l + 1, :]
        m1 = jnp.mean(scaled, axis=-1, keepdims=True)
        m2 = jnp.mean(scaled * standard, axis=-1, keepdims=True)
        return gy[l] + inv[l] * (scaled - m1 - standard * m2)

    def store_weight_grads(l, lo, hi, kind):
        src = 0 if kind == "qkv" else 12
        cols = slice((lo - src) * 128, (hi - src) * 128)
        mine, theirs = (gp, gp_in) if kind == "qkv" else (gy16, gy_in)
        i = 0 if kind == "qkv" else 1
        g = dot_tn(na_own[l, i], mine[l, :, cols]) + dot_tn(na_in[l, i], theirs[l, :, cols])
        for cb in range(lo, hi):
            part = g[:, (cb - lo) * 128 : (cb - lo + 1) * 128].astype(BF16)
            gsend[l, :, :, cb] = part.reshape(n_y, 2, 32, 128)

    def stage1(l):
        out = []
        for k in range(1, n_y):
            yy = (y + k) % n_y
            out.append(remote(gsend.at[l, yy, :, 0:8], r1a.at[l, k - 1], at_y(yy)))
        for k in range(1, 4):
            xx = (x + k) % 4
            out.append(
                remote(
                    gsend.at[l, :, xx // 2, pl.ds(8 + 4 * (xx % 2), 4)],
                    r1b.at[l, k - 1],
                    at_x(xx),
                )
            )
        return out

    def stage2(l, copies):
        out = []
        for c in copies[: n_y - 1]:
            c.wait_recv()
        for i in range(2):
            total = gsend[l, y, i, 0:8].astype(F32)
            for k in range(n_y - 1):
                total = total + r1a[l, k, i].astype(F32)
            acca[l, i] = total.astype(BF16)
        for k in range(1, 4):
            xx = (x + k) % 4
            out.append(
                remote(acca.at[l, xx // 2, pl.ds(4 * (xx % 2), 4)], r2a.at[l, k - 1], at_x(xx))
            )
        for c in copies[n_y - 1 :]:
            c.wait_recv()
        for i in range(n_y):
            total = gsend[l, i, xhi, pl.ds(8 + 4 * xlo, 4)].astype(F32)
            for k in range(3):
                total = total + r1b[l, k, i].astype(F32)
            accb[l, i] = total.astype(BF16)
        for k in range(1, n_y):
            yy = (y + k) % n_y
            out.append(remote(accb.at[l, yy], r2b.at[l, k - 1], at_y(yy)))
        return out

    def stage3(l, copies):
        out = []
        for c in copies:
            c.wait_recv()
        total = acca[l, xhi, pl.ds(4 * xlo, 4)].astype(F32)
        for k in range(3):
            total = total + r2a[l, k].astype(F32)
        acc2[l, 0] = total.reshape(4, 2, 16, 128).astype(BF16)
        total = accb[l, y].astype(F32)
        for k in range(n_y - 1):
            total = total + r2b[l, k].astype(F32)
        acc2[l, 1] = total.reshape(4, 2, 16, 128).astype(BF16)
        for k in range(1, n_z):
            zz = (z + k) % n_z
            out.append(remote(acc2.at[l, :, zz // 2, zz % 2], r3.at[l, k - 1], at_z(zz)))
        return out

    def stage4(l, copies):
        out = []
        for c in copies:
            c.wait_recv()
        for i in range(2):
            total = acc2[l, i, z // 2, z % 2].astype(F32)
            for k in range(n_z - 1):
                total = total + r3[l, k, i].astype(F32)
            fin[l, xlo, i, z // 2, z % 2] = total.astype(BF16)
        mine = fin.at[l, xlo, :, z // 2, z % 2]
        for k in range(1, n_lat):
            i = count[0]
            remote(mine, mine, at((a + k) % n_lat, b))
            s = (a + n_lat - k) % n_lat
            sz = s % n_z
            theirs = fin.at[l, s // n_z, :, sz // 2, sz % 2]
            out.append(expect(i, theirs, theirs, at(s, b)))
        return out

    def finish(l, copies):
        for c in copies:
            c.wait_recv()
        for lo in range(2):
            for i in range(2):
                for cg in range(4):
                    part = fin[l, lo, i, cg].reshape(32, 128).astype(F32)
                    cb = i * 8 + lo * 4 + cg
                    if cb < 12:
                        gq_ref[l, :, cb * 128 : (cb + 1) * 128] = part
                    else:
                        go_ref[l, :, (cb - 12) * 128 : (cb - 11) * 128] = part

    def halo_send(step, field_ref, devices):
        copies = []
        for q in range(3):
            hs[step, q] = field_ref[q * QUAD : q * QUAD + PADQ, :].astype(BF16)
            copies.append(remote(hs.at[step, q], hr.at[step, q], devices[q]))
        return copies

    def halo_take(step, copies, field_ref):
        for q in range(3):
            copies[q].wait_recv()
            field_ref[q * QUAD : (q + 1) * QUAD, :] = hr[step, q].astype(F32)[:QUAD]

    for lev, row, starts in slab_pieces():
        slab = x_ref[lev, row].astype(F32)
        cot = c_ref[lev, row].astype(F32)
        for half in range(2):
            piece = slice(half * 6, half * 6 + 6)
            xs[0, starts[half] : starts[half] + 6, :] = slab[piece]
            gy[1, starts[half] : starts[half] + 6, :] = cot[piece]
    if n_lat > 1:
        last = a == n_lat - 1
    i_id = lax.broadcasted_iota(jnp.int32, (TOK, TOK), 0)
    j_id = lax.broadcasted_iota(jnp.int32, (TOK, TOK), 1)
    cut = jnp.where(last, TOK // 2, TOK)
    same_region = ((i_id < cut) & (j_id < cut)) | ((i_id >= cut) & (j_id >= cut))

    forward(0)
    pl.semaphore_wait(barrier, len(greet))
    cot_copies = halo_send(0, gy.at[1], halo_down)
    middle = xs[0] + dot(att[0], wo_ref[0])
    xs[1] = middle.astype(BF16).astype(F32)
    mid_copies = halo_send(1, xs.at[1], halo_down)
    na_copies = [remote(na_out.at[0], na_in.at[0], partner)]

    halo_take(0, cot_copies, gy.at[1])
    gy16[1] = gy[1].astype(BF16)
    gy_copies = [remote(gy16.at[1], gy_in.at[1], partner)]
    halo_take(1, mid_copies, xs.at[1])
    forward(1)
    na_copies.append(remote(na_out.at[1], na_in.at[1], partner))
    backward_attention(1, 0)
    backward_attention(1, 1)
    xs[1] = backward_input(1).astype(BF16).astype(F32)
    back_copies = halo_send(2, xs.at[1], halo_up)
    gp_copies = [remote(gp.at[1], gp_in.at[1], partner)]
    na_copies[1].wait_recv()
    gy_copies[0].wait_recv()
    store_weight_grads(1, 12, 16, "out")
    gp_copies[0].wait_recv()
    store_weight_grads(1, 0, 12, "qkv")
    s1 = stage1(1)

    gy[0, 3 * QUAD :, :] = xs[1, 3 * QUAD :, :]
    halo_take(2, back_copies, gy.at[0])
    gy16[0] = gy[0].astype(BF16)
    gy_copies.append(remote(gy16.at[0], gy_in.at[0], partner))
    backward_attention(0, 0)
    backward_attention(0, 1)
    gp_copies.append(remote(gp.at[0], gp_in.at[0], partner))
    s2 = stage2(1, s1)
    na_copies[0].wait_recv()
    gy_copies[1].wait_recv()
    store_weight_grads(0, 12, 16, "out")
    gp_copies[1].wait_recv()
    store_weight_grads(0, 0, 12, "qkv")
    t1 = stage1(0)
    s3 = stage3(1, s2)
    out = backward_input(0)
    xs[0] = out
    for lev, row, starts in slab_pieces():
        slab = jnp.concatenate([xs[0, s : s + 6, :] for s in starts], axis=0)
        gx_ref[lev, row] = slab.astype(BF16)

    def gain_step(buf, slot, peers):
        copies = []
        for other, device in peers:
            i = count[0]
            remote(buf.at[slot], buf.at[slot], device)
            copies.append((i, device))
        return copies

    def gain_wait(buf, n, me, copies, sources):
        for (i, device), s in zip(copies, sources):
            expect(i, buf.at[s], buf.at[s], device).wait_recv()
        total = buf[0]
        for j in range(1, n):
            total = total + buf[j]
        return total

    gc = gain_step(gain_c, core, [(1 - core, partner)])
    s4 = stage4(1, s3)
    gain_y[y] = gain_wait(gain_c, 2, core, gc, [1 - core])
    gc = gain_step(gain_y, y, [((y + k) % n_y, at_y((y + k) % n_y)) for k in range(1, n_y)])
    t2 = stage2(0, t1)
    gain_x[x] = gain_wait(gain_y, n_y, y, gc, [(y + n_y - k) % n_y for k in range(1, n_y)])
    gc = gain_step(gain_x, x, [((x + k) % 4, at_x((x + k) % 4)) for k in range(1, 4)])
    finish(1, s4)
    t3 = stage3(0, t2)
    gain_z[z] = gain_wait(gain_x, 4, x, gc, [(x + 4 - k) % 4 for k in range(1, 4)])
    gc = gain_step(gain_z, z, [((z + k) % n_z, at_z((z + k) % n_z)) for k in range(1, n_z)])
    t4 = stage4(0, t3)
    total = gain_wait(gain_z, n_z, z, gc, [(z + n_z - k) % n_z for k in range(1, n_z)])
    for l in range(2):
        for j in range(4):
            gg_ref[l : l + 1, j * 128 : (j + 1) * 128] = total[l * 4 + j : l * 4 + j + 1, :]
    finish(0, t4)
    for copy in pending:
        copy.wait_send()


N_COPIES = 160


def shards(n_lat, n_lon, inputs, cotangent, gains, w_qkv, w_out):
    n_y, n_z = n_lon // 4, n_lat // 2
    vmem = pl.BlockSpec(memory_space=pltpu.VMEM)
    scratch = [
        pltpu.VMEM((2, TOK, D), F32),
        pltpu.VMEM((2, TOK, D), F32),
        pltpu.VMEM((2, TOK, D), F32),
        pltpu.VMEM((2, TOK, 1), F32),
        pltpu.VMEM((2, TOK, 3 * D), BF16),
        pltpu.VMEM((2, 2, STACK, 256), BF16),
        pltpu.VMEM((STACK, 256), BF16),
        pltpu.VMEM((2, 2, STACK, TOK), F32),
        pltpu.VMEM((2, 2, STACK, TOK), BF16),
        pltpu.VMEM((2, TOK, D), BF16),
        pltpu.VMEM((STACK, 256), F32),
        pltpu.VMEM((STACK, TOK), F32),
        pltpu.VMEM((STACK, TOK), BF16),
        pltpu.VMEM((2, TOK, 3 * D), BF16),
        pltpu.VMEM((2, TOK, D), BF16),
        pltpu.VMEM((2, 2, TOK, 256), BF16),
        pltpu.VMEM((2, 2, TOK, 256), BF16),
        pltpu.VMEM((2, 2, TOK, 256), BF16),
        pltpu.VMEM((2, TOK, 3 * D), BF16),
        pltpu.VMEM((2, TOK, D), BF16),
        pltpu.VMEM((3, 3, PADQ, D), BF16),
        pltpu.VMEM((3, 3, PADQ, D), BF16),
        pltpu.VMEM((2, n_y, 2, 16, 32, 128), BF16),
        pltpu.VMEM((2, n_y - 1, 2, 8, 32, 128), BF16),
        pltpu.VMEM((2, 3, n_y, 4, 32, 128), BF16),
        pltpu.VMEM((2, 2, 8, 32, 128), BF16),
        pltpu.VMEM((2, n_y, 4, 32, 128), BF16),
        pltpu.VMEM((2, 3, 4, 32, 128), BF16),
        pltpu.VMEM((2, n_y - 1, 4, 32, 128), BF16),
        pltpu.VMEM((2, 2, 4, 2, 16, 128), BF16),
        pltpu.VMEM((2, n_z - 1, 2, 16, 128), BF16),
        pltpu.VMEM((2, 2, 2, 4, 2, 16, 128), BF16),
        pltpu.VMEM((2, 8, 128), F32),
        pltpu.VMEM((n_y, 8, 128), F32),
        pltpu.VMEM((4, 8, 128), F32),
        pltpu.VMEM((n_z, 8, 128), F32),
        pltpu.SemaphoreType.DMA((N_COPIES,)),
        pltpu.SemaphoreType.DMA((N_COPIES,)),
    ]
    return pl.pallas_call(
        functools.partial(kernel, n_lat, n_lon),
        out_shape=(
            jax.ShapeDtypeStruct(inputs.shape, BF16),
            jax.ShapeDtypeStruct((2, D // n_lon, 3 * D), F32),
            jax.ShapeDtypeStruct((2, D // n_lon, D), F32),
            jax.ShapeDtypeStruct((2, D), F32),
        ),
        in_specs=[vmem] * 5,
        out_specs=(vmem,) * 4,
        scratch_shapes=scratch,
        compiler_params=pltpu.CompilerParams(
            collective_id=0, has_side_effects=True, vmem_limit_bytes=56 * 2**20
        ),
    )(inputs, cotangent, gains, w_qkv, w_out)


def solution(mesh):
    in_specs = (P(None, "lat", "lon", None), P(None, "lat", "lon", None), P(), P(), P())
    out_specs = (P(None, "lat", "lon", None), P(None, "lon", None), P(None, "lon", None), P())
    return jax.shard_map(
        functools.partial(shards, mesh.shape["lat"], mesh.shape["lon"]),
        mesh=mesh,
        in_specs=in_specs,
        out_specs=out_specs,
        check_vma=False,
    )
```

```python
import functools

import jax
import jax.numpy as jnp
import numpy as np
from jax import lax
from jax.experimental import pallas as pl
from jax.experimental.pallas import tpu as pltpu
from jax.sharding import PartitionSpec as P

MESH = pl.DeviceIdType.MESH
F32 = jnp.float32
BF16 = jnp.bfloat16

HEADS = 8
LEV = 2
WLAT = 6
WLON = 12
D = 512
EPS = 1e-05
MASKED = -1e30
TOK = LEV * WLAT * WLON
QUAD = TOK // 4
PADQ = 48
STACK = 4 * TOK


def dot(a, b):
    return lax.dot_general(a, b, (((1,), (0,)), ((), ())), preferred_element_type=F32)


def dot_nt(a, b):
    return lax.dot_general(a, b, (((1,), (1,)), ((), ())), preferred_element_type=F32)


def dot_tn(a, b):
    return lax.dot_general(a, b, (((0,), (0,)), ((), ())), preferred_element_type=F32)


def slab_pieces():
    for row in range(WLAT):
        half_r, r = divmod(row, WLAT // 2)
        for half_c in range(2):
            start = (half_r * 2 + half_c) * QUAD + r * WLON
            yield row, half_c * (WLON // 2), start


def kernel(
    n_lat,
    n_lon,
    x_ref,
    c_ref,
    gains_ref,
    wq_ref,
    wo_ref,
    gx_ref,
    fin_ref,
    gg_ref,
    xs,
    gy,
    std,
    inv,
    proj,
    qm,
    gam,
    probs,
    probs16,
    att,
    tmp,
    scores,
    ds,
    gp,
    gy16,
    na_own,
    na_out,
    na_in,
    gp_in,
    gy_in,
    hs,
    hr,
    gsend,
    r1a,
    r1b,
    acca,
    accb,
    r2a,
    r2b,
    acc2,
    r3,
    fin,
    gain_c,
    gain_y,
    gain_x,
    gain_z,
    send_sem,
    recv_sem,
):
    a = lax.axis_index("lat")
    b = lax.axis_index("lon")
    n_z = n_lat // 2
    n_y = n_lon // 4
    xlo, z = a // n_z, a % n_z
    y, xhi, core = b // 4, (b // 2) % 2, b % 2
    x = xhi * 2 + xlo

    def at(lat, lon):
        return {"lat": lat, "lon": lon}

    def at_x(xx):
        return at((xx % 2) * n_z + z, y * 4 + (xx // 2) * 2 + core)

    def at_y(yy):
        return at(a, yy * 4 + xhi * 2 + core)

    def at_z(zz):
        return at(xlo * n_z + zz, b)

    up_a, dn_a = (a + 1) % n_lat, (a + n_lat - 1) % n_lat
    up_b, dn_b = (b + 1) % n_lon, (b + n_lon - 1) % n_lon
    partner = at(a, y * 4 + xhi * 2 + (1 - core))
    halo_down = [at(dn_a, dn_b), at(dn_a, b), at(a, dn_b)]
    halo_up = [at(up_a, up_b), at(up_a, b), at(a, up_b)]

    greet = halo_down + halo_up + [partner]
    greet += [at_y((y + k) % n_y) for k in range(1, n_y)]
    greet += [at_x((x + k) % 4) for k in range(1, 4)]
    greet += [at((a + k) % n_lat, b) for k in range(1, n_lat)]
    barrier = pltpu.get_barrier_semaphore()
    for device in greet:
        pl.semaphore_signal(barrier, inc=1, device_id=device, device_id_type=MESH)

    count = [0]
    pending = []

    def remote(src, dst, device):
        i = count[0]
        count[0] += 1
        copy = pltpu.make_async_remote_copy(
            src_ref=src,
            dst_ref=dst,
            send_sem=send_sem.at[i],
            recv_sem=recv_sem.at[i],
            device_id=device,
            device_id_type=MESH,
        )
        copy.start()
        pending.append(copy)
        return copy

    def expect(i, src, dst, device):
        return pltpu.make_async_remote_copy(
            src_ref=src,
            dst_ref=dst,
            send_sem=send_sem.at[i],
            recv_sem=recv_sem.at[i],
            device_id=device,
            device_id_type=MESH,
        )

    lane = lax.broadcasted_iota(jnp.int32, (1, 256), 1)
    head_mask = [((lane >= 64 * h) & (lane < 64 * h + 64)).astype(F32) for h in range(4)]
    mask16 = [m.astype(BF16) for m in head_mask]
    scaled16 = [(m * 0.125).astype(BF16) for m in head_mask]

    r_id = lax.broadcasted_iota(jnp.int32, (D, D), 0)
    c_id = lax.broadcasted_iota(jnp.int32, (D, D), 1)
    low = c_id & 255
    which = jnp.where(c_id < 256, core, 1 - core)
    pick = (r_id == ((low >> 5) * 64 + which * 32 + (low & 31))).astype(F32).astype(BF16)

    def select_heads(stacked_ref):
        out = stacked_ref[0:TOK, :] * head_mask[0]
        for h in range(1, 4):
            out = jnp.where(head_mask[h] > 0.5, stacked_ref[h * TOK : (h + 1) * TOK, :], out)
        return out

    def forward(l):
        u = xs[l]
        center = jnp.mean(u, axis=-1, keepdims=True)
        u = u - center
        spread = jnp.mean(u * u, axis=-1, keepdims=True)
        inverse = lax.rsqrt(spread + EPS)
        standard = u * inverse
        std[l] = standard
        inv[l] = inverse
        normed = (standard * gains_ref[l : l + 1, :]).astype(BF16)
        proj[l] = dot(normed, wq_ref[l]).astype(BF16)
        both = dot(normed, pick).astype(BF16)
        na_own[l, 0] = both[:, :256]
        na_out[l, 0] = both[:, 256:]
        for t in range(2):
            q = proj[l, :, 256 * t : 256 * t + 256]
            k = proj[l, :, D + 256 * t : D + 256 * t + 256]
            v = proj[l, :, 2 * D + 256 * t : 2 * D + 256 * t + 256]
            for h in range(4):
                qm[l, t, h * TOK : (h + 1) * TOK, :] = q * scaled16[h]
            scores[...] = dot_nt(qm[l, t], k)
            for h in range(4):
                rows = slice(h * TOK, (h + 1) * TOK)
                s = scores[rows, :]
                if l == 1:
                    s = jnp.where(same_region, s, MASKED)
                e = jnp.exp(s - jnp.max(s, axis=-1, keepdims=True))
                p = e * (1.0 / jnp.sum(e, axis=-1, keepdims=True))
                probs[l, t, rows, :] = p
                probs16[l, t, rows, :] = p.astype(BF16)
            tmp[...] = dot(probs16[l, t], v)
            att[l, :, 256 * t : 256 * t + 256] = select_heads(tmp).astype(BF16)
        both = dot(att[l], pick).astype(BF16)
        na_own[l, 1] = both[:, :256]
        na_out[l, 1] = both[:, 256:]

    def backward_values(l, t):
        cols = slice(256 * t, 256 * t + 256)
        g = dot_nt(gy16[l], wo_ref[l, cols, :]).astype(BF16)
        for h in range(4):
            gam[t, h * TOK : (h + 1) * TOK, :] = g * mask16[h]
        gp[l, :, 2 * D + 256 * t : 2 * D + 256 * t + 256] = dot_tn(probs16[l, t], gam[t]).astype(BF16)

    def backward_scores(l, t):
        k = proj[l, :, D + 256 * t : D + 256 * t + 256]
        v = proj[l, :, 2 * D + 256 * t : 2 * D + 256 * t + 256]
        scores[...] = dot_nt(gam[t], v)
        for h in range(4):
            rows = slice(h * TOK, (h + 1) * TOK)
            p = probs[l, t, rows, :]
            g_p = scores[rows, :]
            total = jnp.sum(g_p * p, axis=-1, keepdims=True)
            ds[rows, :] = (p * (g_p - total)).astype(BF16)
        gp[l, :, D + 256 * t : D + 256 * t + 256] = dot_tn(ds[...], qm[l, t]).astype(BF16)
        tmp[...] = dot(ds[...], k)
        gp[l, :, 256 * t : 256 * t + 256] = (select_heads(tmp) * 0.125).astype(BF16)

    def backward_input(l):
        grad_normed = dot_nt(gp[l], wq_ref[l])
        standard = std[l]
        gain_rows = jnp.sum(grad_normed * standard, axis=0, keepdims=True)
        for j in range(4):
            gain_c[pl.ds(core, 1), l * 4 + j : l * 4 + j + 1, :] = gain_rows[
                :, j * 128 : (j + 1) * 128
            ].reshape(1, 1, 128)
        scaled = grad_normed * gains_ref[l : l + 1, :]
        m1 = jnp.mean(scaled, axis=-1, keepdims=True)
        m2 = jnp.mean(scaled * standard, axis=-1, keepdims=True)
        return gy[l] + inv[l] * (scaled - m1 - standard * m2)

    def send_gp(l, cols):
        return remote(gp.at[l, :, cols], gp_in.at[l, :, cols], partner)

    def weight_grad(l, c, first, i, mine, theirs):
        g = dot_tn(na_own[l, i], mine) + dot_tn(na_in[l, i], theirs)
        for j in range(4):
            part = g[:, j * 128 : (j + 1) * 128].astype(BF16)
            gsend[l, c, :, :, first + j] = part.reshape(n_y, 2, 32, 128)

    def value_out_grads(l):
        weight_grad(l, 0, 4, 1, gy16[l], gy_in[l])
        weight_grad(l, 0, 0, 0, gp[l, :, 2 * D :], gp_in[l, :, 2 * D :])

    def query_key_grads(l):
        weight_grad(l, 1, 0, 0, gp[l, :, :D], gp_in[l, :, :D])
        weight_grad(l, 1, 4, 0, gp[l, :, D : 2 * D], gp_in[l, :, D : 2 * D])

    def stage1(l, c):
        out = []
        for k in range(1, 4):
            if k < n_y:
                yy = (y + k) % n_y
                out.append(remote(gsend.at[l, c, yy, :, 0:4], r1a.at[l, c, k - 1], at_y(yy)))
            xx = (x + k) % 4
            out.append(
                remote(
                    gsend.at[l, c, :, xx // 2, pl.ds(4 + 2 * (xx % 2), 2)],
                    r1b.at[l, c, k - 1],
                    at_x(xx),
                )
            )
        return out

    def stage2(l, c, copies):
        out = []
        for copy in copies:
            copy.wait_recv()
        for i in range(2):
            total = gsend[l, c, y, i, 0:4].astype(F32)
            for k in range(n_y - 1):
                total = total + r1a[l, c, k, i].astype(F32)
            acca[l, c, i] = total.astype(BF16)
        for k in range(1, 4):
            xx = (x + k) % 4
            src = acca.at[l, c, xx // 2, pl.ds(2 * (xx % 2), 2)]
            out.append(remote(src, r2a.at[l, c, k - 1], at_x(xx)))
        for i in range(n_y):
            total = gsend[l, c, i, xhi, pl.ds(4 + 2 * xlo, 2)].astype(F32)
            for k in range(3):
                total = total + r1b[l, c, k, i].astype(F32)
            accb[l, c, i] = total.astype(BF16)
        for k in range(1, n_y):
            yy = (y + k) % n_y
            out.append(remote(accb.at[l, c, yy], r2b.at[l, c, k - 1], at_y(yy)))
        return out

    def stage3_sum(l, c, copies):
        for copy in copies:
            copy.wait_recv()
        total = acca[l, c, xhi, pl.ds(2 * xlo, 2)].astype(F32)
        for k in range(3):
            total = total + r2a[l, c, k].astype(F32)
        acc2[l, c, 0:2] = total.reshape(2, 2, 16, 128).astype(BF16)
        total = accb[l, c, y].astype(F32)
        for k in range(n_y - 1):
            total = total + r2b[l, c, k].astype(F32)
        acc2[l, c, 2:4] = total.reshape(2, 2, 16, 128).astype(BF16)

    def stage3(l):
        out = []
        for k in range(1, n_z):
            zz = (z + k) % n_z
            out.append(remote(acc2.at[l, :, zz // 2, zz % 2], r3.at[l, k - 1], at_z(zz)))
        return out

    def stage4(l, copies):
        out = []
        for copy in copies:
            copy.wait_recv()
        total = acc2[l, :, z // 2, z % 2].astype(F32)
        for k in range(n_z - 1):
            total = total + r3[l, k].astype(F32)
        fin[l, xlo, :, z // 2, z % 2] = total.astype(BF16)
        mine = fin.at[l, xlo, :, z // 2, z % 2]
        for k in range(1, n_lat):
            i = count[0]
            remote(mine, mine, at((a + k) % n_lat, b))
            s = (a + n_lat - k) % n_lat
            sz = s % n_z
            theirs = fin.at[l, s // n_z, :, sz // 2, sz % 2]
            out.append(expect(i, theirs, theirs, at(s, b)))
        return out

    def finish(l, copies):
        for copy in copies:
            copy.wait_recv()
        fin_ref[l] = fin[l]

    def halo_send(step, field_ref, devices):
        copies = []
        for q in range(3):
            hs[step, q] = field_ref[q * QUAD : q * QUAD + PADQ, :].astype(BF16)
            copies.append(remote(hs.at[step, q], hr.at[step, q], devices[q]))
        return copies

    def halo_take(step, copies, field_ref):
        for q in range(3):
            copies[q].wait_recv()
            field_ref[q * QUAD : (q + 1) * QUAD, :] = hr[step, q].astype(F32)[:QUAD]

    for row, col, start in slab_pieces():
        cols = slice(col, col + WLON // 2)
        xs[0, start : start + WLON, :] = x_ref[row, cols].astype(F32).reshape(WLON, D)
        gy[1, start : start + WLON, :] = c_ref[row, cols].astype(F32).reshape(WLON, D)
    last = a == n_lat - 1
    i_id = lax.broadcasted_iota(jnp.int32, (TOK, TOK), 0)
    j_id = lax.broadcasted_iota(jnp.int32, (TOK, TOK), 1)
    cut = jnp.where(last, TOK // 2, TOK)
    same_region = ((i_id < cut) & (j_id < cut)) | ((i_id >= cut) & (j_id >= cut))

    forward(0)
    pl.semaphore_wait(barrier, len(greet))
    cot_copies = halo_send(0, gy.at[1], halo_down)
    middle = xs[0] + dot(att[0], wo_ref[0])
    xs[1] = middle.astype(BF16).astype(F32)
    mid_copies = halo_send(1, xs.at[1], halo_down)
    na_copies = [remote(na_out.at[0], na_in.at[0], partner)]

    halo_take(0, cot_copies, gy.at[1])
    gy16[1] = gy[1].astype(BF16)
    gy_copies = [remote(gy16.at[1], gy_in.at[1], partner)]
    halo_take(1, mid_copies, xs.at[1])
    forward(1)
    na_copies.append(remote(na_out.at[1], na_in.at[1], partner))
    backward_values(1, 0)
    backward_values(1, 1)
    v_copies = [send_gp(1, slice(2 * D, 3 * D))]
    backward_scores(1, 0)
    backward_scores(1, 1)
    qk_copies = [send_gp(1, slice(0, 2 * D))]
    xs[1] = backward_input(1).astype(BF16).astype(F32)
    back_copies = halo_send(2, xs.at[1], halo_up)
    gy[0, 3 * QUAD :, :] = xs[1, 3 * QUAD :, :]
    na_copies[1].wait_recv()
    gy_copies[0].wait_recv()
    v_copies[0].wait_recv()
    value_out_grads(1)
    s1v = stage1(1, 0)
    qk_copies[0].wait_recv()
    query_key_grads(1)
    s1q = stage1(1, 1)

    halo_take(2, back_copies, gy.at[0])
    gy16[0] = gy[0].astype(BF16)
    gy_copies.append(remote(gy16.at[0], gy_in.at[0], partner))
    backward_values(0, 0)
    backward_values(0, 1)
    v_copies.append(send_gp(0, slice(2 * D, 3 * D)))
    backward_scores(0, 0)
    na_copies[0].wait_recv()
    gy_copies[1].wait_recv()
    v_copies[1].wait_recv()
    value_out_grads(0)
    t1v = stage1(0, 0)
    backward_scores(0, 1)
    qk_copies.append(send_gp(0, slice(0, 2 * D)))
    s2v = stage2(1, 0, s1v)
    qk_copies[1].wait_recv()
    query_key_grads(0)
    t1q = stage1(0, 1)
    s2q = stage2(1, 1, s1q)
    xs[0] = backward_input(0)
    for row, col, start in slab_pieces():
        piece = xs[0, start : start + WLON, :].reshape(WLON // 2, LEV, D)
        gx_ref[row, col : col + WLON // 2] = piece.astype(BF16)

    def gain_step(buf, slot, peers):
        copies = []
        for other, device in peers:
            i = count[0]
            remote(buf.at[slot], buf.at[slot], device)
            copies.append((i, device))
        return copies

    def gain_wait(buf, n, me, copies, sources):
        for (i, device), s in zip(copies, sources):
            expect(i, buf.at[s], buf.at[s], device).wait_recv()
        total = buf[0]
        for j in range(1, n):
            total = total + buf[j]
        return total

    gc = gain_step(gain_c, core, [(1 - core, partner)])
    t2v = stage2(0, 0, t1v)
    stage3_sum(1, 0, s2v)
    stage3_sum(1, 1, s2q)
    s3 = stage3(1)
    gain_y[y] = gain_wait(gain_c, 2, core, gc, [1 - core])
    gc = gain_step(gain_y, y, [((y + k) % n_y, at_y((y + k) % n_y)) for k in range(1, n_y)])
    t2q = stage2(0, 1, t1q)
    gain_x[x] = gain_wait(gain_y, n_y, y, gc, [(y + n_y - k) % n_y for k in range(1, n_y)])
    gc = gain_step(gain_x, x, [((x + k) % 4, at_x((x + k) % 4)) for k in range(1, 4)])
    stage3_sum(0, 0, t2v)
    stage3_sum(0, 1, t2q)
    t3 = stage3(0)
    gain_z[z] = gain_wait(gain_x, 4, x, gc, [(x + 4 - k) % 4 for k in range(1, 4)])
    gc = gain_step(gain_z, z, [((z + k) % n_z, at_z((z + k) % n_z)) for k in range(1, n_z)])
    s4 = stage4(1, s3)
    t4 = stage4(0, t3)
    total = gain_wait(gain_z, n_z, z, gc, [(z + n_z - k) % n_z for k in range(1, n_z)])
    for l in range(2):
        for j in range(4):
            gg_ref[l : l + 1, j * 128 : (j + 1) * 128] = total[l * 4 + j : l * 4 + j + 1, :]
    finish(1, s4)
    finish(0, t4)
    for copy in pending:
        copy.wait_send()


def unpack(gx_ref, fin_ref, gg_ref, gx_out, gq_out, go_out, gg_out):
    gx_out[...] = gx_ref[...]
    gg_out[...] = gg_ref[...]
    for l in range(2):
        for lo in range(2):
            for j in range(2):
                cols = slice((2 * lo + j) * 128, (2 * lo + j + 1) * 128)
                block = [
                    [fin_ref[l, lo, c, 2 * h + j].reshape(32, 128).astype(F32) for h in range(2)]
                    for c in range(2)
                ]
                gq_out[l, :, cols] = block[1][0]
                gq_out[l, :, D + cols.start : D + cols.stop] = block[1][1]
                gq_out[l, :, 2 * D + cols.start : 2 * D + cols.stop] = block[0][0]
                go_out[l, :, cols] = block[0][1]


N_COPIES = 170


def shards(n_lat, n_lon, inputs, cotangent, gains, w_qkv, w_out):
    n_y, n_z = n_lon // 4, n_lat // 2
    vmem = pl.BlockSpec(memory_space=pltpu.VMEM)
    scratch = [
        pltpu.VMEM((2, TOK, D), F32),
        pltpu.VMEM((2, TOK, D), F32),
        pltpu.VMEM((2, TOK, D), F32),
        pltpu.VMEM((2, TOK, 1), F32),
        pltpu.VMEM((2, TOK, 3 * D), BF16),
        pltpu.VMEM((2, 2, STACK, 256), BF16),
        pltpu.VMEM((2, STACK, 256), BF16),
        pltpu.VMEM((2, 2, STACK, TOK), F32),
        pltpu.VMEM((2, 2, STACK, TOK), BF16),
        pltpu.VMEM((2, TOK, D), BF16),
        pltpu.VMEM((STACK, 256), F32),
        pltpu.VMEM((STACK, TOK), F32),
        pltpu.VMEM((STACK, TOK), BF16),
        pltpu.VMEM((2, TOK, 3 * D), BF16),
        pltpu.VMEM((2, TOK, D), BF16),
        pltpu.VMEM((2, 2, TOK, 256), BF16),
        pltpu.VMEM((2, 2, TOK, 256), BF16),
        pltpu.VMEM((2, 2, TOK, 256), BF16),
        pltpu.VMEM((2, TOK, 3 * D), BF16),
        pltpu.VMEM((2, TOK, D), BF16),
        pltpu.VMEM((3, 3, PADQ, D), BF16),
        pltpu.VMEM((3, 3, PADQ, D), BF16),
        pltpu.VMEM((2, 2, n_y, 2, 8, 32, 128), BF16),
        pltpu.VMEM((2, 2, n_y - 1, 2, 4, 32, 128), BF16),
        pltpu.VMEM((2, 2, 3, n_y, 2, 32, 128), BF16),
        pltpu.VMEM((2, 2, 2, 4, 32, 128), BF16),
        pltpu.VMEM((2, 2, n_y, 2, 32, 128), BF16),
        pltpu.VMEM((2, 2, 3, 2, 32, 128), BF16),
        pltpu.VMEM((2, 2, n_y - 1, 2, 32, 128), BF16),
        pltpu.VMEM((2, 2, 4, 2, 16, 128), BF16),
        pltpu.VMEM((2, n_z - 1, 2, 16, 128), BF16),
        pltpu.VMEM((2, 2, 2, 4, 2, 16, 128), BF16),
        pltpu.VMEM((2, 8, 128), F32),
        pltpu.VMEM((n_y, 8, 128), F32),
        pltpu.VMEM((4, 8, 128), F32),
        pltpu.VMEM((n_z, 8, 128), F32),
        pltpu.SemaphoreType.DMA((N_COPIES,)),
        pltpu.SemaphoreType.DMA((N_COPIES,)),
    ]
    swap = (1, 2, 0, 3)
    gx, fin, gg = pl.pallas_call(
        functools.partial(kernel, n_lat, n_lon),
        out_shape=(
            jax.ShapeDtypeStruct((WLAT, WLON, LEV, D), BF16),
            jax.ShapeDtypeStruct((2, 2, 2, 4, 2, 16, 128), BF16),
            jax.ShapeDtypeStruct((2, D), F32),
        ),
        in_specs=[vmem] * 5,
        out_specs=(vmem,) * 3,
        scratch_shapes=scratch,
        compiler_params=pltpu.CompilerParams(
            collective_id=0, has_side_effects=True, vmem_limit_bytes=56 * 2**20
        ),
    )(inputs.transpose(swap), cotangent.transpose(swap), gains, w_qkv, w_out)
    gx, gq, go, gg = pl.pallas_call(
        unpack,
        out_shape=(
            jax.ShapeDtypeStruct(gx.shape, BF16),
            jax.ShapeDtypeStruct((2, D // n_lon, 3 * D), F32),
            jax.ShapeDtypeStruct((2, D // n_lon, D), F32),
            jax.ShapeDtypeStruct((2, D), F32),
        ),
        in_specs=[vmem] * 3,
        out_specs=(vmem,) * 4,
    )(gx, fin, gg)
    return gx.transpose(2, 0, 1, 3), gq, go, gg


def solution(mesh):
    in_specs = (P(None, "lat", "lon", None), P(None, "lat", "lon", None), P(), P(), P())
    out_specs = (P(None, "lat", "lon", None), P(None, "lon", None), P(None, "lon", None), P())
    return jax.shard_map(
        functools.partial(shards, mesh.shape["lat"], mesh.shape["lon"]),
        mesh=mesh,
        in_specs=in_specs,
        out_specs=out_specs,
        check_vma=False,
    )
```

```python
import functools

import jax
import jax.numpy as jnp
import numpy as np
from jax import lax
from jax.experimental import pallas as pl
from jax.experimental.pallas import tpu as pltpu
from jax.sharding import PartitionSpec as P

MESH = pl.DeviceIdType.MESH
F32 = jnp.float32
BF16 = jnp.bfloat16

HEADS = 8
LEV = 2
WLAT = 6
WLON = 12
D = 512
EPS = 1e-05
MASKED = -1e30
TOK = LEV * WLAT * WLON
QUAD = TOK // 4
PADQ = 48
STACK = 4 * TOK


def dot(a, b):
    return lax.dot_general(a, b, (((1,), (0,)), ((), ())), preferred_element_type=F32)


def dot_nt(a, b):
    return lax.dot_general(a, b, (((1,), (1,)), ((), ())), preferred_element_type=F32)


def dot_tn(a, b):
    return lax.dot_general(a, b, (((0,), (0,)), ((), ())), preferred_element_type=F32)


def slab_pieces():
    for row in range(WLAT):
        half_r, r = divmod(row, WLAT // 2)
        for half_c in range(2):
            start = (half_r * 2 + half_c) * QUAD + r * WLON
            yield row, half_c * (WLON // 2), start


def kernel(
    n_lat,
    n_lon,
    x_hbm,
    c_hbm,
    gains_hbm,
    wq_hbm,
    wo_hbm,
    gx_hbm,
    fin_ref,
    gg_ref,
    x_ref,
    c_ref,
    gains_ref,
    wq_ref,
    wo_ref,
    gx_ref,
    xs,
    gy,
    std,
    inv,
    proj,
    qm,
    gam,
    probs,
    probs16,
    att,
    tmp,
    scores,
    ds,
    gp,
    gy16,
    na_own,
    na_out,
    na_in,
    gp_in,
    gy_in,
    hs,
    hr,
    gsend,
    r1a,
    r1b,
    acca,
    accb,
    r2a,
    r2b,
    acc2,
    r3,
    own4,
    r4,
    normed_ref,
    gain_c,
    gain_y,
    gain_x,
    gain_z,
    send_sem,
    recv_sem,
    local_sem,
):
    a = lax.axis_index("lat")
    b = lax.axis_index("lon")
    n_z = n_lat // 2
    n_y = n_lon // 4
    xlo, z = a // n_z, a % n_z
    y, xhi, core = b // 4, (b // 2) % 2, b % 2
    x = xhi * 2 + xlo

    def at(lat, lon):
        return {"lat": lat, "lon": lon}

    def at_x(xx):
        return at((xx % 2) * n_z + z, y * 4 + (xx // 2) * 2 + core)

    def at_y(yy):
        return at(a, yy * 4 + xhi * 2 + core)

    def at_z(zz):
        return at(xlo * n_z + zz, b)

    up_a, dn_a = (a + 1) % n_lat, (a + n_lat - 1) % n_lat
    up_b, dn_b = (b + 1) % n_lon, (b + n_lon - 1) % n_lon
    partner = at(a, y * 4 + xhi * 2 + (1 - core))
    halo_down = [at(dn_a, dn_b), at(dn_a, b), at(a, dn_b)]
    halo_up = [at(up_a, up_b), at(up_a, b), at(a, up_b)]

    greet = halo_down + halo_up + [partner]
    greet += [at_y((y + k) % n_y) for k in range(1, n_y)]
    greet += [at_x((x + k) % 4) for k in range(1, 4)]
    greet += [at((a + k) % n_lat, b) for k in range(1, n_lat)]
    barrier = pltpu.get_barrier_semaphore()
    for device in greet:
        pl.semaphore_signal(barrier, inc=1, device_id=device, device_id_type=MESH)

    def local(i, src, dst):
        copy = pltpu.make_async_copy(src, dst, local_sem.at[i])
        copy.start()
        return copy

    loads = [
        local(0, x_hbm, x_ref),
        local(1, gains_hbm, gains_ref),
        local(2, wq_hbm.at[0], wq_ref.at[0]),
        local(3, wo_hbm.at[0], wo_ref.at[0]),
        local(4, c_hbm, c_ref),
        local(5, wq_hbm.at[1], wq_ref.at[1]),
        local(6, wo_hbm.at[1], wo_ref.at[1]),
    ]

    pending = []

    def remote(whole, copies):
        i = len(pending)

        def describe(src, dst, device):
            return pltpu.make_async_remote_copy(
                src_ref=src,
                dst_ref=dst,
                send_sem=send_sem.at[i],
                recv_sem=recv_sem.at[i],
                device_id=device,
                device_id_type=MESH,
            )

        for src, dst, device in copies:
            describe(src, dst, device).start()
        pending.append(describe(whole, whole, partner))
        return pending[i]

    def to_partner(src, dst):
        return remote(dst, [(src, dst, partner)])

    lane = lax.broadcasted_iota(jnp.int32, (1, 256), 1)
    head_mask = [((lane >= 64 * h) & (lane < 64 * h + 64)).astype(F32) for h in range(4)]
    mask16 = [m.astype(BF16) for m in head_mask]
    scaled16 = [(m * 0.125).astype(BF16) for m in head_mask]

    r_id = lax.broadcasted_iota(jnp.int32, (D, D), 0)
    c_id = lax.broadcasted_iota(jnp.int32, (D, D), 1)
    low = c_id & 255
    which = jnp.where(c_id < 256, core, 1 - core)
    pick = (r_id == ((low >> 5) * 64 + which * 32 + (low & 31))).astype(F32).astype(BF16)

    def select_heads(stacked_ref):
        out = stacked_ref[0:TOK, :] * head_mask[0]
        for h in range(1, 4):
            out = jnp.where(head_mask[h] > 0.5, stacked_ref[h * TOK : (h + 1) * TOK, :], out)
        return out

    def forward(l):
        u = xs[l]
        center = jnp.mean(u, axis=-1, keepdims=True)
        u = u - center
        spread = jnp.mean(u * u, axis=-1, keepdims=True)
        inverse = lax.rsqrt(spread + EPS)
        standard = u * inverse
        std[l] = standard
        inv[l] = inverse
        normed = (standard * gains_ref[l : l + 1, :]).astype(BF16)
        loads[2 if l == 0 else 5].wait()
        proj[l] = dot(normed, wq_ref[l]).astype(BF16)
        normed_ref[l] = normed
        for t in range(2):
            q = proj[l, :, 256 * t : 256 * t + 256]
            k = proj[l, :, D + 256 * t : D + 256 * t + 256]
            v = proj[l, :, 2 * D + 256 * t : 2 * D + 256 * t + 256]
            for h in range(4):
                qm[l, t, h * TOK : (h + 1) * TOK, :] = q * scaled16[h]
            scores[...] = dot_nt(qm[l, t], k)
            for h in range(4):
                rows = slice(h * TOK, (h + 1) * TOK)
                s = scores[rows, :]
                if l == 1:
                    s = jnp.where(same_region, s, MASKED)
                e = jnp.exp(s - jnp.max(s, axis=-1, keepdims=True))
                p = e * (1.0 / jnp.sum(e, axis=-1, keepdims=True))
                probs[l, t, rows, :] = p
                probs16[l, t, rows, :] = p.astype(BF16)
            tmp[...] = dot(probs16[l, t], v)
            att[l, :, 256 * t : 256 * t + 256] = select_heads(tmp).astype(BF16)

    def share_rows(l):
        for i, rows in enumerate((normed_ref, att)):
            both = dot(rows[l], pick).astype(BF16)
            na_own[l, i] = both[:, :256]
            na_out[l, i] = both[:, 256:]
        return to_partner(na_out.at[l], na_in.at[l])

    def backward_values(l, t):
        cols = slice(256 * t, 256 * t + 256)
        g = dot_nt(gy16[l], wo_ref[l, cols, :]).astype(BF16)
        for h in range(4):
            gam[t, h * TOK : (h + 1) * TOK, :] = g * mask16[h]
        gp[l, :, 2 * D + 256 * t : 2 * D + 256 * t + 256] = dot_tn(probs16[l, t], gam[t]).astype(BF16)

    def backward_scores(l, t):
        k = proj[l, :, D + 256 * t : D + 256 * t + 256]
        v = proj[l, :, 2 * D + 256 * t : 2 * D + 256 * t + 256]
        scores[...] = dot_nt(gam[t], v)
        for h in range(4):
            rows = slice(h * TOK, (h + 1) * TOK)
            p = probs[l, t, rows, :]
            g_p = scores[rows, :]
            total = jnp.sum(g_p * p, axis=-1, keepdims=True)
            ds[rows, :] = (p * (g_p - total)).astype(BF16)
        gp[l, :, D + 256 * t : D + 256 * t + 256] = dot_tn(ds[...], qm[l, t]).astype(BF16)
        tmp[...] = dot(ds[...], k)
        gp[l, :, 256 * t : 256 * t + 256] = (select_heads(tmp) * 0.125).astype(BF16)

    def backward_input(l):
        grad_normed = dot_nt(gp[l], wq_ref[l])
        standard = std[l]
        gain_rows = jnp.sum(grad_normed * standard, axis=0, keepdims=True)
        for j in range(4):
            gain_c[0, l * 4 + j : l * 4 + j + 1, :] = gain_rows[:, j * 128 : (j + 1) * 128]
        scaled = grad_normed * gains_ref[l : l + 1, :]
        m1 = jnp.mean(scaled, axis=-1, keepdims=True)
        m2 = jnp.mean(scaled * standard, axis=-1, keepdims=True)
        return gy[l] + inv[l] * (scaled - m1 - standard * m2)

    def send_gp(l, cols):
        return to_partner(gp.at[l, :, cols], gp_in.at[l, :, cols])

    def weight_grad(l, c, first, i, mine, theirs):
        g = dot_tn(na_own[l, i], mine) + dot_tn(na_in[l, i], theirs)
        for j in range(4):
            part = g[:, j * 128 : (j + 1) * 128].astype(BF16)
            gsend[l, c, :, :, first + j] = part.reshape(n_y, 2, 32, 128)

    def value_out_grads(l):
        weight_grad(l, 0, 4, 1, gy16[l], gy_in[l])
        weight_grad(l, 0, 0, 0, gp[l, :, 2 * D :], gp_in[l, :, 2 * D :])

    def query_key_grads(l):
        weight_grad(l, 1, 0, 0, gp[l, :, :D], gp_in[l, :, :D])
        weight_grad(l, 1, 4, 0, gp[l, :, D : 2 * D], gp_in[l, :, D : 2 * D])

    def stage1(l, c):
        over_y, over_x = [], []
        for k in range(1, 4):
            if k < n_y:
                yy = (y + k) % n_y
                over_y.append((gsend.at[l, c, yy, :, 0:4], r1a.at[l, c, k - 1], at_y(yy)))
            xx = (x + k) % 4
            src = gsend.at[l, c, :, xx // 2, pl.ds(4 + 2 * (xx % 2), 2)]
            over_x.append((src, r1b.at[l, c, k - 1], at_x(xx)))
        return remote(r1a.at[l, c], over_y), remote(r1b.at[l, c], over_x)

    def stage2(l, c, copies):
        copies[0].wait_recv()
        for i in range(2):
            total = gsend[l, c, y, i, 0:4].astype(F32)
            for k in range(n_y - 1):
                total = total + r1a[l, c, k, i].astype(F32)
            acca[l, c, i] = total.astype(BF16)
        over_x = []
        for k in range(1, 4):
            xx = (x + k) % 4
            src = acca.at[l, c, xx // 2, pl.ds(2 * (xx % 2), 2)]
            over_x.append((src, r2a.at[l, c, k - 1], at_x(xx)))
        over_x = remote(r2a.at[l, c], over_x)
        copies[1].wait_recv()
        for i in range(n_y):
            total = gsend[l, c, i, xhi, pl.ds(4 + 2 * xlo, 2)].astype(F32)
            for k in range(3):
                total = total + r1b[l, c, k, i].astype(F32)
            accb[l, c, i] = total.astype(BF16)
        over_y = []
        for k in range(1, n_y):
            yy = (y + k) % n_y
            over_y.append((accb.at[l, c, yy], r2b.at[l, c, k - 1], at_y(yy)))
        return over_x, remote(r2b.at[l, c], over_y)

    def stage3_sum(l, c, copies):
        for copy in copies:
            copy.wait_recv()
        total = acca[l, c, xhi, pl.ds(2 * xlo, 2)].astype(F32)
        for k in range(3):
            total = total + r2a[l, c, k].astype(F32)
        acc2[l, c, 0:2] = total.reshape(2, 2, 16, 128).astype(BF16)
        total = accb[l, c, y].astype(F32)
        for k in range(n_y - 1):
            total = total + r2b[l, c, k].astype(F32)
        acc2[l, c, 2:4] = total.reshape(2, 2, 16, 128).astype(BF16)

    def stage3(l):
        over_z = []
        for k in range(1, n_z):
            zz = (z + k) % n_z
            over_z.append((acc2.at[l, :, zz // 2, zz % 2], r3.at[l, k - 1], at_z(zz)))
        return remote(r3.at[l], over_z)

    def stage4(l, copies):
        copies.wait_recv()
        total = acc2[l, :, z // 2, z % 2].astype(F32)
        for k in range(n_z - 1):
            total = total + r3[l, k].astype(F32)
        own4[l] = total.astype(BF16)
        over_lat = []
        for k in range(1, n_lat):
            over_lat.append((own4.at[l], r4.at[l, k - 1], at((a + k) % n_lat, b)))
        return remote(r4.at[l], over_lat)

    def finish(l, copies):
        fin_ref[l, xlo, :, z // 2, z % 2] = own4[l]
        copies.wait_recv()
        for k in range(1, n_lat):
            source = (a + n_lat - k) % n_lat
            zz = source % n_z
            fin_ref[l, source // n_z, :, zz // 2, zz % 2] = r4[l, k - 1]

    def halo_send(step, field_ref, devices):
        copies = []
        for q in range(3):
            hs[step, q] = field_ref[q * QUAD : q * QUAD + PADQ, :].astype(BF16)
            copies.append((hs.at[step, q], hr.at[step, q], devices[q]))
        return remote(hr.at[step], copies)

    def halo_take(step, copies, field_ref):
        copies.wait_recv()
        for q in range(3):
            field_ref[q * QUAD : (q + 1) * QUAD, :] = hr[step, q].astype(F32)[:QUAD]

    loads[0].wait()
    for row, col, start in slab_pieces():
        cols = slice(col, col + WLON // 2)
        xs[0, start : start + WLON, :] = x_ref[row, cols].astype(F32).reshape(WLON, D)
    loads[1].wait()
    last = a == n_lat - 1
    i_id = lax.broadcasted_iota(jnp.int32, (TOK, TOK), 0)
    j_id = lax.broadcasted_iota(jnp.int32, (TOK, TOK), 1)
    cut = jnp.where(last, TOK // 2, TOK)
    same_region = ((i_id < cut) & (j_id < cut)) | ((i_id >= cut) & (j_id >= cut))

    forward(0)
    loads[3].wait()
    middle = xs[0] + dot(att[0], wo_ref[0])
    xs[1] = middle.astype(BF16).astype(F32)
    pl.semaphore_wait(barrier, len(greet))
    mid_copies = halo_send(1, xs.at[1], halo_down)
    loads[4].wait()
    for row, col, start in slab_pieces():
        cols = slice(col, col + WLON // 2)
        gy[1, start : start + WLON, :] = c_ref[row, cols].astype(F32).reshape(WLON, D)
    cot_copies = halo_send(0, gy.at[1], halo_down)
    na_copies = [share_rows(0)]

    halo_take(1, mid_copies, xs.at[1])
    forward(1)
    halo_take(0, cot_copies, gy.at[1])
    gy16[1] = gy[1].astype(BF16)
    gy_copies = [to_partner(gy16.at[1], gy_in.at[1])]
    loads[6].wait()
    backward_values(1, 0)
    backward_values(1, 1)
    v_copies = [send_gp(1, slice(2 * D, 3 * D))]
    backward_scores(1, 0)
    backward_scores(1, 1)
    qk_copies = [send_gp(1, slice(0, 2 * D))]
    xs[1] = backward_input(1).astype(BF16).astype(F32)
    back_copies = halo_send(2, xs.at[1], halo_up)
    gy[0, 3 * QUAD :, :] = xs[1, 3 * QUAD :, :]
    na_copies.append(share_rows(1))
    na_copies[1].wait_recv()
    gy_copies[0].wait_recv()
    v_copies[0].wait_recv()
    value_out_grads(1)
    s1v = stage1(1, 0)
    qk_copies[0].wait_recv()
    query_key_grads(1)
    s1q = stage1(1, 1)

    halo_take(2, back_copies, gy.at[0])
    gy16[0] = gy[0].astype(BF16)
    gy_copies.append(to_partner(gy16.at[0], gy_in.at[0]))
    backward_values(0, 0)
    backward_values(0, 1)
    v_copies.append(send_gp(0, slice(2 * D, 3 * D)))
    backward_scores(0, 0)
    na_copies[0].wait_recv()
    gy_copies[1].wait_recv()
    v_copies[1].wait_recv()
    value_out_grads(0)
    t1v = stage1(0, 0)
    backward_scores(0, 1)
    qk_copies.append(send_gp(0, slice(0, 2 * D)))
    s2v = stage2(1, 0, s1v)
    qk_copies[1].wait_recv()
    query_key_grads(0)
    t1q = stage1(0, 1)
    s2q = stage2(1, 1, s1q)
    xs[0] = backward_input(0)
    for row, col, start in slab_pieces():
        piece = xs[0, start : start + WLON, :].reshape(WLON // 2, LEV, D)
        gx_ref[row, col : col + WLON // 2] = piece.astype(BF16)
    stores = [local(7, gx_ref, gx_hbm)]

    def gain_send(buf, peers):
        return remote(
            buf.at[pl.ds(1, len(peers))],
            [(buf.at[0], buf.at[k + 1], device) for k, device in enumerate(peers)],
        )

    def gain_sum(buf, copies, me, n):
        copies.wait_recv()
        total = buf[me]
        for j in range(1, n):
            total = total + buf[(me + n - j) % n]
        return total

    g1 = gain_send(gain_c, [partner])
    t2v = stage2(0, 0, t1v)
    stage3_sum(1, 0, s2v)
    stage3_sum(1, 1, s2q)
    s3 = stage3(1)
    gain_y[0] = gain_sum(gain_c, g1, core, 2)
    g2 = gain_send(gain_y, [at_y((y + k) % n_y) for k in range(1, n_y)])
    t2q = stage2(0, 1, t1q)
    gain_x[0] = gain_sum(gain_y, g2, y, n_y)
    g3 = gain_send(gain_x, [at_x((x + k) % 4) for k in range(1, 4)])
    stage3_sum(0, 0, t2v)
    stage3_sum(0, 1, t2q)
    t3 = stage3(0)
    gain_z[0] = gain_sum(gain_x, g3, x, 4)
    g4 = gain_send(gain_z, [at_z((z + k) % n_z) for k in range(1, n_z)])
    s4 = stage4(1, s3)
    t4 = stage4(0, t3)
    total = gain_sum(gain_z, g4, z, n_z)
    for l in range(2):
        for j in range(4):
            gg_ref[l : l + 1, j * 128 : (j + 1) * 128] = total[l * 4 + j : l * 4 + j + 1, :]
    finish(1, s4)
    finish(0, t4)
    stores[0].wait()
    for copy in pending:
        copy.wait_send()


def unpack(gx_ref, fin_ref, gg_ref, gx_out, gq_out, go_out, gg_out):
    gx_out[...] = gx_ref[...]
    gg_out[...] = gg_ref[...]
    for l in range(2):
        for lo in range(2):
            for j in range(2):
                cols = slice((2 * lo + j) * 128, (2 * lo + j + 1) * 128)
                block = [
                    [fin_ref[l, lo, c, 2 * h + j].reshape(32, 128).astype(F32) for h in range(2)]
                    for c in range(2)
                ]
                gq_out[l, :, cols] = block[1][0]
                gq_out[l, :, D + cols.start : D + cols.stop] = block[1][1]
                gq_out[l, :, 2 * D + cols.start : 2 * D + cols.stop] = block[0][0]
                go_out[l, :, cols] = block[0][1]


N_GROUPS = 35


def shards(n_lat, n_lon, inputs, cotangent, gains, w_qkv, w_out):
    n_y, n_z = n_lon // 4, n_lat // 2
    vmem = pl.BlockSpec(memory_space=pltpu.VMEM)
    hbm = pl.BlockSpec(memory_space=pl.ANY)
    scratch = [
        pltpu.VMEM((WLAT, WLON, LEV, D), BF16),
        pltpu.VMEM((WLAT, WLON, LEV, D), BF16),
        pltpu.VMEM((2, D), F32),
        pltpu.VMEM((2, D, 3 * D), BF16),
        pltpu.VMEM((2, D, D), BF16),
        pltpu.VMEM((WLAT, WLON, LEV, D), BF16),
        pltpu.VMEM((2, TOK, D), F32),
        pltpu.VMEM((2, TOK, D), F32),
        pltpu.VMEM((2, TOK, D), F32),
        pltpu.VMEM((2, TOK, 1), F32),
        pltpu.VMEM((2, TOK, 3 * D), BF16),
        pltpu.VMEM((2, 2, STACK, 256), BF16),
        pltpu.VMEM((2, STACK, 256), BF16),
        pltpu.VMEM((2, 2, STACK, TOK), F32),
        pltpu.VMEM((2, 2, STACK, TOK), BF16),
        pltpu.VMEM((2, TOK, D), BF16),
        pltpu.VMEM((STACK, 256), F32),
        pltpu.VMEM((STACK, TOK), F32),
        pltpu.VMEM((STACK, TOK), BF16),
        pltpu.VMEM((2, TOK, 3 * D), BF16),
        pltpu.VMEM((2, TOK, D), BF16),
        pltpu.VMEM((2, 2, TOK, 256), BF16),
        pltpu.VMEM((2, 2, TOK, 256), BF16),
        pltpu.VMEM((2, 2, TOK, 256), BF16),
        pltpu.VMEM((2, TOK, 3 * D), BF16),
        pltpu.VMEM((2, TOK, D), BF16),
        pltpu.VMEM((3, 3, PADQ, D), BF16),
        pltpu.VMEM((3, 3, PADQ, D), BF16),
        pltpu.VMEM((2, 2, n_y, 2, 8, 32, 128), BF16),
        pltpu.VMEM((2, 2, n_y - 1, 2, 4, 32, 128), BF16),
        pltpu.VMEM((2, 2, 3, n_y, 2, 32, 128), BF16),
        pltpu.VMEM((2, 2, 2, 4, 32, 128), BF16),
        pltpu.VMEM((2, 2, n_y, 2, 32, 128), BF16),
        pltpu.VMEM((2, 2, 3, 2, 32, 128), BF16),
        pltpu.VMEM((2, 2, n_y - 1, 2, 32, 128), BF16),
        pltpu.VMEM((2, 2, 4, 2, 16, 128), BF16),
        pltpu.VMEM((2, n_z - 1, 2, 16, 128), BF16),
        pltpu.VMEM((2, 2, 16, 128), BF16),
        pltpu.VMEM((2, n_lat - 1, 2, 16, 128), BF16),
        pltpu.VMEM((2, TOK, D), BF16),
        pltpu.VMEM((2, 8, 128), F32),
        pltpu.VMEM((n_y, 8, 128), F32),
        pltpu.VMEM((4, 8, 128), F32),
        pltpu.VMEM((n_z, 8, 128), F32),
        pltpu.SemaphoreType.DMA((N_GROUPS,)),
        pltpu.SemaphoreType.DMA((N_GROUPS,)),
        pltpu.SemaphoreType.DMA((8,)),
    ]
    swap = (1, 2, 0, 3)
    gx, fin, gg = pl.pallas_call(
        functools.partial(kernel, n_lat, n_lon),
        out_shape=(
            jax.ShapeDtypeStruct((WLAT, WLON, LEV, D), BF16),
            jax.ShapeDtypeStruct((2, 2, 2, 4, 2, 16, 128), BF16),
            jax.ShapeDtypeStruct((2, D), F32),
        ),
        in_specs=[hbm] * 5,
        out_specs=(hbm, vmem, vmem),
        scratch_shapes=scratch,
        compiler_params=pltpu.CompilerParams(
            collective_id=0, has_side_effects=True, vmem_limit_bytes=56 * 2**20
        ),
    )(inputs.transpose(swap), cotangent.transpose(swap), gains, w_qkv, w_out)
    gx, gq, go, gg = pl.pallas_call(
        unpack,
        out_shape=(
            jax.ShapeDtypeStruct(gx.shape, BF16),
            jax.ShapeDtypeStruct((2, D // n_lon, 3 * D), F32),
            jax.ShapeDtypeStruct((2, D // n_lon, D), F32),
            jax.ShapeDtypeStruct((2, D), F32),
        ),
        in_specs=[vmem] * 3,
        out_specs=(vmem,) * 4,
    )(gx, fin, gg)
    return gx.transpose(2, 0, 1, 3), gq, go, gg


def solution(mesh):
    in_specs = (P(None, "lat", "lon", None), P(None, "lat", "lon", None), P(), P(), P())
    out_specs = (P(None, "lat", "lon", None), P(None, "lon", None), P(None, "lon", None), P())
    return jax.shard_map(
        functools.partial(shards, mesh.shape["lat"], mesh.shape["lon"]),
        mesh=mesh,
        in_specs=in_specs,
        out_specs=out_specs,
        check_vma=False,
    )
```

```python
import functools

import jax
import jax.numpy as jnp
import numpy as np
from jax import lax
from jax.experimental import pallas as pl
from jax.experimental.pallas import tpu as pltpu
from jax.sharding import PartitionSpec as P

MESH = pl.DeviceIdType.MESH
F32 = jnp.float32
BF16 = jnp.bfloat16

HEADS = 8
LEV = 2
WLAT = 6
WLON = 12
D = 512
EPS = 1e-05
MASKED = -1e30
TOK = LEV * WLAT * WLON
QUAD = TOK // 4
PADQ = 48
STACK = 4 * TOK


def dot(a, b):
    return lax.dot_general(a, b, (((1,), (0,)), ((), ())), preferred_element_type=F32)


def dot_nt(a, b):
    return lax.dot_general(a, b, (((1,), (1,)), ((), ())), preferred_element_type=F32)


def dot_tn(a, b):
    return lax.dot_general(a, b, (((0,), (0,)), ((), ())), preferred_element_type=F32)


def far_first(n):
    return sorted(range(1, n), key=lambda k: -min(k, n - k))


def slab_pieces():
    for row in range(WLAT):
        half_r, r = divmod(row, WLAT // 2)
        for half_c in range(2):
            start = (half_r * 2 + half_c) * QUAD + r * WLON
            yield row, half_c * (WLON // 2), start


def kernel(
    n_lat,
    n_lon,
    x_hbm,
    c_hbm,
    gains_hbm,
    wq_hbm,
    wo_hbm,
    gx_hbm,
    fin_ref,
    gg_ref,
    x_ref,
    c_ref,
    gains_ref,
    wq_ref,
    wo_ref,
    gx_ref,
    xs,
    gy,
    std,
    inv,
    proj,
    qm,
    gam,
    probs,
    probs16,
    att,
    tmp,
    scores,
    ds,
    gp,
    gy16,
    na_own,
    na_out,
    na_in,
    gp_in,
    gy_in,
    hs,
    hr,
    gsend,
    r1a,
    r1b,
    acca,
    accb,
    r2a,
    r2b,
    acc2,
    r3,
    own4,
    r4,
    normed_ref,
    part_g,
    gain_c,
    gain_y,
    gain_x,
    gain_z,
    send_sem,
    recv_sem,
    local_sem,
):
    a = lax.axis_index("lat")
    b = lax.axis_index("lon")
    n_z = n_lat // 2
    n_y = n_lon // 4
    xlo, z = a // n_z, a % n_z
    y, xhi, core = b // 4, (b // 2) % 2, b % 2
    x = xhi * 2 + xlo

    def at(lat, lon):
        return {"lat": lat, "lon": lon}

    def at_x(xx):
        return at((xx % 2) * n_z + z, y * 4 + (xx // 2) * 2 + core)

    def at_y(yy):
        return at(a, yy * 4 + xhi * 2 + core)

    def at_z(zz):
        return at(xlo * n_z + zz, b)

    up_a, dn_a = (a + 1) % n_lat, (a + n_lat - 1) % n_lat
    up_b, dn_b = (b + 1) % n_lon, (b + n_lon - 1) % n_lon
    partner = at(a, y * 4 + xhi * 2 + (1 - core))
    halo_down = [at(dn_a, dn_b), at(dn_a, b), at(a, dn_b)]
    halo_up = [at(up_a, up_b), at(up_a, b), at(a, up_b)]

    greet = halo_down + halo_up + [partner]
    greet += [at_y((y + k) % n_y) for k in range(1, n_y)]
    greet += [at_x((x + k) % 4) for k in range(1, 4)]
    greet = [at((a + k) % n_lat, b) for k in far_first(n_lat)] + greet
    barrier = pltpu.get_barrier_semaphore()
    for device in greet:
        pl.semaphore_signal(barrier, inc=1, device_id=device, device_id_type=MESH)

    def local(i, src, dst):
        copy = pltpu.make_async_copy(src, dst, local_sem.at[i])
        copy.start()
        return copy

    loads = [
        local(0, x_hbm, x_ref),
        local(1, gains_hbm, gains_ref),
        local(2, wq_hbm.at[0], wq_ref.at[0]),
        local(3, wo_hbm.at[0], wo_ref.at[0]),
        local(4, c_hbm, c_ref),
        local(5, wq_hbm.at[1], wq_ref.at[1]),
        local(6, wo_hbm.at[1], wo_ref.at[1]),
    ]

    pending = []

    def remote(whole, copies):
        i = len(pending)

        def describe(src, dst, device):
            return pltpu.make_async_remote_copy(
                src_ref=src,
                dst_ref=dst,
                send_sem=send_sem.at[i],
                recv_sem=recv_sem.at[i],
                device_id=device,
                device_id_type=MESH,
            )

        for src, dst, device in copies:
            describe(src, dst, device).start()
        pending.append(describe(whole, whole, partner))
        return pending[i]

    def to_partner(src, dst):
        return remote(dst, [(src, dst, partner)])

    lane = lax.broadcasted_iota(jnp.int32, (1, 256), 1)
    head_mask = [((lane >= 64 * h) & (lane < 64 * h + 64)).astype(F32) for h in range(4)]
    mask16 = [m.astype(BF16) for m in head_mask]
    scaled16 = [(m * 0.125).astype(BF16) for m in head_mask]

    r_id = lax.broadcasted_iota(jnp.int32, (D, D), 0)
    c_id = lax.broadcasted_iota(jnp.int32, (D, D), 1)
    low = c_id & 255
    which = jnp.where(c_id < 256, core, 1 - core)
    pick = (r_id == ((low >> 5) * 64 + which * 32 + (low & 31))).astype(F32).astype(BF16)

    def select_heads(stacked_ref):
        out = stacked_ref[0:TOK, :] * head_mask[0]
        for h in range(1, 4):
            out = jnp.where(head_mask[h] > 0.5, stacked_ref[h * TOK : (h + 1) * TOK, :], out)
        return out

    def forward(l):
        u = xs[l]
        center = jnp.mean(u, axis=-1, keepdims=True)
        u = u - center
        spread = jnp.mean(u * u, axis=-1, keepdims=True)
        inverse = lax.rsqrt(spread + EPS)
        standard = u * inverse
        std[l] = standard
        inv[l] = inverse
        normed = (standard * gains_ref[l : l + 1, :]).astype(BF16)
        loads[2 if l == 0 else 5].wait()
        proj[l] = dot(normed, wq_ref[l]).astype(BF16)
        normed_ref[l] = normed
        for t in range(2):
            q = proj[l, :, 256 * t : 256 * t + 256]
            k = proj[l, :, D + 256 * t : D + 256 * t + 256]
            v = proj[l, :, 2 * D + 256 * t : 2 * D + 256 * t + 256]
            for h in range(4):
                qm[l, t, h * TOK : (h + 1) * TOK, :] = q * scaled16[h]
            scores[...] = dot_nt(qm[l, t], k)
            for h in range(4):
                rows = slice(h * TOK, (h + 1) * TOK)
                s = scores[rows, :]
                if l == 1:
                    s = jnp.where(same_region, s, MASKED)
                e = jnp.exp(s - jnp.max(s, axis=-1, keepdims=True))
                p = e * (1.0 / jnp.sum(e, axis=-1, keepdims=True))
                probs[l, t, rows, :] = p
                probs16[l, t, rows, :] = p.astype(BF16)
            tmp[...] = dot(probs16[l, t], v)
            att[l, :, 256 * t : 256 * t + 256] = select_heads(tmp).astype(BF16)

    def share_rows(l):
        for i, rows in enumerate((normed_ref, att)):
            both = dot(rows[l], pick).astype(BF16)
            na_own[l, i] = both[:, :256]
            na_out[l, i] = both[:, 256:]
        return to_partner(na_out.at[l], na_in.at[l])

    def backward_values(l, t):
        cols = slice(256 * t, 256 * t + 256)
        g = dot_nt(gy16[l], wo_ref[l, cols, :]).astype(BF16)
        for h in range(4):
            gam[t, h * TOK : (h + 1) * TOK, :] = g * mask16[h]
        gp[l, :, 2 * D + 256 * t : 2 * D + 256 * t + 256] = dot_tn(probs16[l, t], gam[t]).astype(BF16)

    def backward_scores(l, t):
        k = proj[l, :, D + 256 * t : D + 256 * t + 256]
        v = proj[l, :, 2 * D + 256 * t : 2 * D + 256 * t + 256]
        scores[...] = dot_nt(gam[t], v)
        for h in range(4):
            rows = slice(h * TOK, (h + 1) * TOK)
            p = probs[l, t, rows, :]
            g_p = scores[rows, :]
            total = jnp.sum(g_p * p, axis=-1, keepdims=True)
            ds[rows, :] = (p * (g_p - total)).astype(BF16)
        gp[l, :, D + 256 * t : D + 256 * t + 256] = dot_tn(ds[...], qm[l, t]).astype(BF16)
        tmp[...] = dot(ds[...], k)
        gp[l, :, 256 * t : 256 * t + 256] = (select_heads(tmp) * 0.125).astype(BF16)

    def backward_input(l):
        grad_normed = dot_nt(gp[l], wq_ref[l])
        standard = std[l]
        gain_rows = jnp.sum(grad_normed * standard, axis=0, keepdims=True)
        for j in range(4):
            gain_c[0, l * 4 + j : l * 4 + j + 1, :] = gain_rows[:, j * 128 : (j + 1) * 128]
        scaled = grad_normed * gains_ref[l : l + 1, :]
        m1 = jnp.mean(scaled, axis=-1, keepdims=True)
        m2 = jnp.mean(scaled * standard, axis=-1, keepdims=True)
        return gy[l] + inv[l] * (scaled - m1 - standard * m2)

    def send_gp(l, cols):
        return to_partner(gp.at[l, :, cols], gp_in.at[l, :, cols])

    def weight_grad(l, c, first, i, mine, theirs):
        g = dot_tn(na_own[l, i], mine) + dot_tn(na_in[l, i], theirs)
        for j in range(4):
            part = g[:, j * 128 : (j + 1) * 128].astype(BF16)
            gsend[l, c, :, :, first + j] = part.reshape(n_y, 2, 32, 128)

    def value_out_grads(l):
        weight_grad(l, 0, 4, 1, gy16[l], gy_in[l])
        weight_grad(l, 0, 0, 0, gp[l, :, 2 * D :], gp_in[l, :, 2 * D :])

    def query_key_own(l):
        part_g[...] = dot_tn(na_own[l, 0], gp[l, :, : 2 * D])

    def query_key_grads(l):
        g = part_g[...] + dot_tn(na_in[l, 0], gp_in[l, :, : 2 * D])
        for j in range(8):
            part = g[:, j * 128 : (j + 1) * 128].astype(BF16)
            gsend[l, 1, :, :, j] = part.reshape(n_y, 2, 32, 128)

    def stage1(l, c):
        over_y, over_x = [], []
        for k in far_first(4):
            if k < n_y:
                yy = (y + k) % n_y
                over_y.append((gsend.at[l, c, yy, :, 0:4], r1a.at[l, c, k - 1], at_y(yy)))
            xx = (x + k) % 4
            src = gsend.at[l, c, :, xx // 2, pl.ds(4 + 2 * (xx % 2), 2)]
            over_x.append((src, r1b.at[l, c, k - 1], at_x(xx)))
        return remote(r1a.at[l, c], over_y), remote(r1b.at[l, c], over_x)

    def stage2(l, c, copies):
        copies[0].wait_recv()
        for i in range(2):
            total = gsend[l, c, y, i, 0:4].astype(F32)
            for k in range(n_y - 1):
                total = total + r1a[l, c, k, i].astype(F32)
            acca[l, c, i] = total.astype(BF16)
        over_x = []
        for k in far_first(4):
            xx = (x + k) % 4
            src = acca.at[l, c, xx // 2, pl.ds(2 * (xx % 2), 2)]
            over_x.append((src, r2a.at[l, c, k - 1], at_x(xx)))
        over_x = remote(r2a.at[l, c], over_x)
        copies[1].wait_recv()
        for i in range(n_y):
            total = gsend[l, c, i, xhi, pl.ds(4 + 2 * xlo, 2)].astype(F32)
            for k in range(3):
                total = total + r1b[l, c, k, i].astype(F32)
            accb[l, c, i] = total.astype(BF16)
        over_y = []
        for k in far_first(n_y):
            yy = (y + k) % n_y
            over_y.append((accb.at[l, c, yy], r2b.at[l, c, k - 1], at_y(yy)))
        return over_x, remote(r2b.at[l, c], over_y)

    def stage3_sum(l, c, copies):
        for copy in copies:
            copy.wait_recv()
        total = acca[l, c, xhi, pl.ds(2 * xlo, 2)].astype(F32)
        for k in range(3):
            total = total + r2a[l, c, k].astype(F32)
        acc2[l, c, 0:2] = total.reshape(2, 2, 16, 128).astype(BF16)
        total = accb[l, c, y].astype(F32)
        for k in range(n_y - 1):
            total = total + r2b[l, c, k].astype(F32)
        acc2[l, c, 2:4] = total.reshape(2, 2, 16, 128).astype(BF16)

    def stage3(l):
        over_z = []
        for k in far_first(n_z):
            zz = (z + k) % n_z
            over_z.append((acc2.at[l, :, zz // 2, zz % 2], r3.at[l, k - 1], at_z(zz)))
        return remote(r3.at[l], over_z)

    def stage4(l, copies):
        copies.wait_recv()
        total = acc2[l, :, z // 2, z % 2].astype(F32)
        for k in range(n_z - 1):
            total = total + r3[l, k].astype(F32)
        own4[l] = total.astype(BF16)
        over_lat = []
        for k in sorted(range(1, n_lat), key=lambda k: -min(k % n_z, n_z - k % n_z)):
            over_lat.append((own4.at[l], r4.at[l, k - 1], at((a + k) % n_lat, b)))
        return remote(r4.at[l], over_lat)

    def finish(l, copies):
        fin_ref[l, xlo, :, z // 2, z % 2] = own4[l]
        copies.wait_recv()
        for k in range(1, n_lat):
            source = (a + n_lat - k) % n_lat
            zz = source % n_z
            fin_ref[l, source // n_z, :, zz // 2, zz % 2] = r4[l, k - 1]

    def halo_send(step, field_ref, devices):
        copies = []
        for q in range(3):
            hs[step, q] = field_ref[q * QUAD : q * QUAD + PADQ, :].astype(BF16)
            copies.append((hs.at[step, q], hr.at[step, q], devices[q]))
        return remote(hr.at[step], copies)

    def halo_take(step, copies, field_ref):
        copies.wait_recv()
        for q in range(3):
            field_ref[q * QUAD : (q + 1) * QUAD, :] = hr[step, q].astype(F32)[:QUAD]

    loads[0].wait()
    for row, col, start in slab_pieces():
        cols = slice(col, col + WLON // 2)
        xs[0, start : start + WLON, :] = x_ref[row, cols].astype(F32).reshape(WLON, D)
    loads[1].wait()
    last = a == n_lat - 1
    i_id = lax.broadcasted_iota(jnp.int32, (TOK, TOK), 0)
    j_id = lax.broadcasted_iota(jnp.int32, (TOK, TOK), 1)
    cut = jnp.where(last, TOK // 2, TOK)
    same_region = ((i_id < cut) & (j_id < cut)) | ((i_id >= cut) & (j_id >= cut))

    forward(0)
    loads[3].wait()
    middle = xs[0] + dot(att[0], wo_ref[0])
    xs[1] = middle.astype(BF16).astype(F32)
    pl.semaphore_wait(barrier, len(greet))
    mid_copies = halo_send(1, xs.at[1], halo_down)
    loads[4].wait()
    for row, col, start in slab_pieces():
        cols = slice(col, col + WLON // 2)
        gy[1, start : start + WLON, :] = c_ref[row, cols].astype(F32).reshape(WLON, D)
    cot_copies = halo_send(0, gy.at[1], halo_down)
    na_copies = [share_rows(0)]

    halo_take(1, mid_copies, xs.at[1])
    forward(1)
    halo_take(0, cot_copies, gy.at[1])
    gy16[1] = gy[1].astype(BF16)
    gy_copies = [to_partner(gy16.at[1], gy_in.at[1])]
    loads[6].wait()
    backward_values(1, 0)
    backward_values(1, 1)
    v_copies = [send_gp(1, slice(2 * D, 3 * D))]
    backward_scores(1, 0)
    backward_scores(1, 1)
    qk_copies = [send_gp(1, slice(0, 2 * D))]
    xs[1] = backward_input(1).astype(BF16).astype(F32)
    back_copies = halo_send(2, xs.at[1], halo_up)
    gy[0, 3 * QUAD :, :] = xs[1, 3 * QUAD :, :]
    na_copies.append(share_rows(1))
    na_copies[1].wait_recv()
    gy_copies[0].wait_recv()
    v_copies[0].wait_recv()
    value_out_grads(1)
    s1v = stage1(1, 0)
    query_key_own(1)
    qk_copies[0].wait_recv()
    query_key_grads(1)
    s1q = stage1(1, 1)

    halo_take(2, back_copies, gy.at[0])
    gy16[0] = gy[0].astype(BF16)
    gy_copies.append(to_partner(gy16.at[0], gy_in.at[0]))
    backward_values(0, 0)
    backward_values(0, 1)
    v_copies.append(send_gp(0, slice(2 * D, 3 * D)))
    backward_scores(0, 0)
    na_copies[0].wait_recv()
    gy_copies[1].wait_recv()
    v_copies[1].wait_recv()
    value_out_grads(0)
    t1v = stage1(0, 0)
    backward_scores(0, 1)
    qk_copies.append(send_gp(0, slice(0, 2 * D)))
    s2v = stage2(1, 0, s1v)
    query_key_own(0)
    qk_copies[1].wait_recv()
    query_key_grads(0)
    t1q = stage1(0, 1)
    s2q = stage2(1, 1, s1q)
    xs[0] = backward_input(0)
    for row, col, start in slab_pieces():
        piece = xs[0, start : start + WLON, :].reshape(WLON // 2, LEV, D)
        gx_ref[row, col : col + WLON // 2] = piece.astype(BF16)
    stores = [local(7, gx_ref, gx_hbm)]

    def gain_send(buf, peers):
        return remote(
            buf.at[pl.ds(1, len(peers))],
            [(buf.at[0], buf.at[k + 1], device) for k, device in enumerate(peers)],
        )

    def gain_sum(buf, copies, me, n):
        copies.wait_recv()
        total = buf[me]
        for j in range(1, n):
            total = total + buf[(me + n - j) % n]
        return total

    g1 = gain_send(gain_c, [partner])
    t2v = stage2(0, 0, t1v)
    stage3_sum(1, 0, s2v)
    stage3_sum(1, 1, s2q)
    s3 = stage3(1)
    gain_y[0] = gain_sum(gain_c, g1, core, 2)
    g2 = gain_send(gain_y, [at_y((y + k) % n_y) for k in range(1, n_y)])
    t2q = stage2(0, 1, t1q)
    gain_x[0] = gain_sum(gain_y, g2, y, n_y)
    g3 = gain_send(gain_x, [at_x((x + k) % 4) for k in range(1, 4)])
    stage3_sum(0, 0, t2v)
    stage3_sum(0, 1, t2q)
    t3 = stage3(0)
    s4 = stage4(1, s3)
    gain_z[0] = gain_sum(gain_x, g3, x, 4)
    g4 = gain_send(gain_z, [at_z((z + k) % n_z) for k in range(1, n_z)])
    t4 = stage4(0, t3)
    total = gain_sum(gain_z, g4, z, n_z)
    for l in range(2):
        for j in range(4):
            gg_ref[l : l + 1, j * 128 : (j + 1) * 128] = total[l * 4 + j : l * 4 + j + 1, :]
    finish(1, s4)
    finish(0, t4)
    stores[0].wait()
    for copy in pending:
        copy.wait_send()


def unpack(gx_ref, fin_ref, gg_ref, gx_out, gq_out, go_out, gg_out):
    gx_out[...] = gx_ref[...]
    gg_out[...] = gg_ref[...]
    for l in range(2):
        for lo in range(2):
            for j in range(2):
                cols = slice((2 * lo + j) * 128, (2 * lo + j + 1) * 128)
                block = [
                    [fin_ref[l, lo, c, 2 * h + j].reshape(32, 128).astype(F32) for h in range(2)]
                    for c in range(2)
                ]
                gq_out[l, :, cols] = block[1][0]
                gq_out[l, :, D + cols.start : D + cols.stop] = block[1][1]
                gq_out[l, :, 2 * D + cols.start : 2 * D + cols.stop] = block[0][0]
                go_out[l, :, cols] = block[0][1]


N_GROUPS = 35


def shards(n_lat, n_lon, inputs, cotangent, gains, w_qkv, w_out):
    n_y, n_z = n_lon // 4, n_lat // 2
    vmem = pl.BlockSpec(memory_space=pltpu.VMEM)
    hbm = pl.BlockSpec(memory_space=pl.ANY)
    scratch = [
        pltpu.VMEM((WLAT, WLON, LEV, D), BF16),
        pltpu.VMEM((WLAT, WLON, LEV, D), BF16),
        pltpu.VMEM((2, D), F32),
        pltpu.VMEM((2, D, 3 * D), BF16),
        pltpu.VMEM((2, D, D), BF16),
        pltpu.VMEM((WLAT, WLON, LEV, D), BF16),
        pltpu.VMEM((2, TOK, D), F32),
        pltpu.VMEM((2, TOK, D), F32),
        pltpu.VMEM((2, TOK, D), F32),
        pltpu.VMEM((2, TOK, 1), F32),
        pltpu.VMEM((2, TOK, 3 * D), BF16),
        pltpu.VMEM((2, 2, STACK, 256), BF16),
        pltpu.VMEM((2, STACK, 256), BF16),
        pltpu.VMEM((2, 2, STACK, TOK), F32),
        pltpu.VMEM((2, 2, STACK, TOK), BF16),
        pltpu.VMEM((2, TOK, D), BF16),
        pltpu.VMEM((STACK, 256), F32),
        pltpu.VMEM((STACK, TOK), F32),
        pltpu.VMEM((STACK, TOK), BF16),
        pltpu.VMEM((2, TOK, 3 * D), BF16),
        pltpu.VMEM((2, TOK, D), BF16),
        pltpu.VMEM((2, 2, TOK, 256), BF16),
        pltpu.VMEM((2, 2, TOK, 256), BF16),
        pltpu.VMEM((2, 2, TOK, 256), BF16),
        pltpu.VMEM((2, TOK, 3 * D), BF16),
        pltpu.VMEM((2, TOK, D), BF16),
        pltpu.VMEM((3, 3, PADQ, D), BF16),
        pltpu.VMEM((3, 3, PADQ, D), BF16),
        pltpu.VMEM((2, 2, n_y, 2, 8, 32, 128), BF16),
        pltpu.VMEM((2, 2, n_y - 1, 2, 4, 32, 128), BF16),
        pltpu.VMEM((2, 2, 3, n_y, 2, 32, 128), BF16),
        pltpu.VMEM((2, 2, 2, 4, 32, 128), BF16),
        pltpu.VMEM((2, 2, n_y, 2, 32, 128), BF16),
        pltpu.VMEM((2, 2, 3, 2, 32, 128), BF16),
        pltpu.VMEM((2, 2, n_y - 1, 2, 32, 128), BF16),
        pltpu.VMEM((2, 2, 4, 2, 16, 128), BF16),
        pltpu.VMEM((2, n_z - 1, 2, 16, 128), BF16),
        pltpu.VMEM((2, 2, 16, 128), BF16),
        pltpu.VMEM((2, n_lat - 1, 2, 16, 128), BF16),
        pltpu.VMEM((2, TOK, D), BF16),
        pltpu.VMEM((D // 2, 2 * D), F32),
        pltpu.VMEM((2, 8, 128), F32),
        pltpu.VMEM((n_y, 8, 128), F32),
        pltpu.VMEM((4, 8, 128), F32),
        pltpu.VMEM((n_z, 8, 128), F32),
        pltpu.SemaphoreType.DMA((N_GROUPS,)),
        pltpu.SemaphoreType.DMA((N_GROUPS,)),
        pltpu.SemaphoreType.DMA((8,)),
    ]
    swap = (1, 2, 0, 3)
    gx, fin, gg = pl.pallas_call(
        functools.partial(kernel, n_lat, n_lon),
        out_shape=(
            jax.ShapeDtypeStruct((WLAT, WLON, LEV, D), BF16),
            jax.ShapeDtypeStruct((2, 2, 2, 4, 2, 16, 128), BF16),
            jax.ShapeDtypeStruct((2, D), F32),
        ),
        in_specs=[hbm] * 5,
        out_specs=(hbm, vmem, vmem),
        scratch_shapes=scratch,
        compiler_params=pltpu.CompilerParams(
            collective_id=0, has_side_effects=True, vmem_limit_bytes=56 * 2**20
        ),
    )(inputs.transpose(swap), cotangent.transpose(swap), gains, w_qkv, w_out)
    gx, gq, go, gg = pl.pallas_call(
        unpack,
        out_shape=(
            jax.ShapeDtypeStruct(gx.shape, BF16),
            jax.ShapeDtypeStruct((2, D // n_lon, 3 * D), F32),
            jax.ShapeDtypeStruct((2, D // n_lon, D), F32),
            jax.ShapeDtypeStruct((2, D), F32),
        ),
        in_specs=[vmem] * 3,
        out_specs=(vmem,) * 4,
    )(gx, fin, gg)
    return gx.transpose(2, 0, 1, 3), gq, go, gg


def solution(mesh):
    in_specs = (P(None, "lat", "lon", None), P(None, "lat", "lon", None), P(), P(), P())
    out_specs = (P(None, "lat", "lon", None), P(None, "lon", None), P(None, "lon", None), P())
    return jax.shard_map(
        functools.partial(shards, mesh.shape["lat"], mesh.shape["lon"]),
        mesh=mesh,
        in_specs=in_specs,
        out_specs=out_specs,
        check_vma=False,
    )
```

```python
import functools

import jax
import jax.numpy as jnp
import numpy as np
from jax import lax
from jax.experimental import pallas as pl
from jax.experimental.pallas import tpu as pltpu
from jax.sharding import PartitionSpec as P

MESH = pl.DeviceIdType.MESH
F32 = jnp.float32
BF16 = jnp.bfloat16

HEADS = 8
LEV = 2
WLAT = 6
WLON = 12
D = 512
EPS = 1e-05
MASKED = -1e30
TOK = LEV * WLAT * WLON
QUAD = TOK // 4
PADQ = 48
STACK = 4 * TOK


def dot(a, b):
    return lax.dot_general(a, b, (((1,), (0,)), ((), ())), preferred_element_type=F32)


def dot_nt(a, b):
    return lax.dot_general(a, b, (((1,), (1,)), ((), ())), preferred_element_type=F32)


def dot_tn(a, b):
    return lax.dot_general(a, b, (((0,), (0,)), ((), ())), preferred_element_type=F32)


def far_first(n):
    return sorted(range(1, n), key=lambda k: -min(k, n - k))


def slab_pieces():
    for row in range(WLAT):
        half_r, r = divmod(row, WLAT // 2)
        for half_c in range(2):
            start = (half_r * 2 + half_c) * QUAD + r * WLON
            yield row, half_c * (WLON // 2), start


def kernel(
    n_lat,
    n_lon,
    x_hbm,
    c_hbm,
    gains_hbm,
    wq_hbm,
    wo_hbm,
    gx_hbm,
    fin_ref,
    gg_ref,
    x_ref,
    c_ref,
    gains_ref,
    wq_ref,
    wo_ref,
    gx_ref,
    xs,
    gy,
    std,
    inv,
    proj,
    qm,
    gam,
    probs,
    probs16,
    att,
    tmp,
    scores,
    ds,
    gp,
    gy16,
    na_own,
    na_out,
    na_in,
    gp_in,
    gy_in,
    hs,
    hr,
    gsend,
    r1a,
    r1b,
    acca,
    accb,
    r2a,
    r2b,
    acc2,
    r3,
    own4,
    r4,
    normed_ref,
    part_g,
    gain_c,
    gain_y,
    gain_x,
    gain_z,
    send_sem,
    recv_sem,
    local_sem,
):
    a = lax.axis_index("lat")
    b = lax.axis_index("lon")
    n_z = n_lat // 2
    n_y = n_lon // 4
    xlo, z = a // n_z, a % n_z
    y, xhi, core = b // 4, (b // 2) % 2, b % 2
    x = xhi * 2 + xlo

    def at(lat, lon):
        return {"lat": lat, "lon": lon}

    def at_x(xx):
        return at((xx % 2) * n_z + z, y * 4 + (xx // 2) * 2 + core)

    def at_y(yy):
        return at(a, yy * 4 + xhi * 2 + core)

    def at_z(zz):
        return at(xlo * n_z + zz, b)

    up_a, dn_a = (a + 1) % n_lat, (a + n_lat - 1) % n_lat
    up_b, dn_b = (b + 1) % n_lon, (b + n_lon - 1) % n_lon
    partner = at(a, y * 4 + xhi * 2 + (1 - core))
    halo_down = [at(dn_a, dn_b), at(dn_a, b), at(a, dn_b)]
    halo_up = [at(up_a, up_b), at(up_a, b), at(a, up_b)]

    def local(i, src, dst):
        copy = pltpu.make_async_copy(src, dst, local_sem.at[i])
        copy.start()
        return copy

    loads = [local(0, x_hbm, x_ref), local(1, gains_hbm, gains_ref)]
    loads.append(local(2, wq_hbm.at[0], wq_ref.at[0]))

    greet = halo_down + halo_up + [partner]
    greet += [at_y((y + k) % n_y) for k in range(1, n_y)]
    greet += [at_x((x + k) % 4) for k in range(1, 4)]
    greet = [at((a + k) % n_lat, b) for k in far_first(n_lat)] + greet
    barrier = pltpu.get_barrier_semaphore()
    for device in greet:
        pl.semaphore_signal(barrier, inc=1, device_id=device, device_id_type=MESH)

    loads += [
        local(3, wo_hbm.at[0], wo_ref.at[0]),
        local(4, c_hbm, c_ref),
        local(5, wq_hbm.at[1], wq_ref.at[1]),
        local(6, wo_hbm.at[1], wo_ref.at[1]),
    ]

    pending = []

    def remote(whole, copies):
        i = len(pending)

        def describe(src, dst, device):
            return pltpu.make_async_remote_copy(
                src_ref=src,
                dst_ref=dst,
                send_sem=send_sem.at[i],
                recv_sem=recv_sem.at[i],
                device_id=device,
                device_id_type=MESH,
            )

        for src, dst, device in copies:
            describe(src, dst, device).start()
        pending.append(describe(whole, whole, partner))
        return pending[i]

    def to_partner(src, dst):
        return remote(dst, [(src, dst, partner)])

    lane = lax.broadcasted_iota(jnp.int32, (1, 256), 1)
    head_mask = [((lane >= 64 * h) & (lane < 64 * h + 64)).astype(F32) for h in range(4)]
    mask16 = [m.astype(BF16) for m in head_mask]
    scaled16 = [(m * 0.125).astype(BF16) for m in head_mask]

    r_id = lax.broadcasted_iota(jnp.int32, (D, D), 0)
    c_id = lax.broadcasted_iota(jnp.int32, (D, D), 1)
    low = c_id & 255
    which = jnp.where(c_id < 256, core, 1 - core)
    pick = (r_id == ((low >> 5) * 64 + which * 32 + (low & 31))).astype(F32).astype(BF16)

    def select_heads(stacked_ref):
        out = stacked_ref[0:TOK, :] * head_mask[0]
        for h in range(1, 4):
            out = jnp.where(head_mask[h] > 0.5, stacked_ref[h * TOK : (h + 1) * TOK, :], out)
        return out

    def forward(l):
        u = xs[l]
        center = jnp.mean(u, axis=-1, keepdims=True)
        u = u - center
        spread = jnp.mean(u * u, axis=-1, keepdims=True)
        inverse = lax.rsqrt(spread + EPS)
        standard = u * inverse
        std[l] = standard
        inv[l] = inverse
        normed = (standard * gains_ref[l : l + 1, :]).astype(BF16)
        loads[2 if l == 0 else 5].wait()
        proj[l] = dot(normed, wq_ref[l]).astype(BF16)
        normed_ref[l] = normed
        for t in range(2):
            q = proj[l, :, 256 * t : 256 * t + 256]
            k = proj[l, :, D + 256 * t : D + 256 * t + 256]
            v = proj[l, :, 2 * D + 256 * t : 2 * D + 256 * t + 256]
            for h in range(4):
                qm[l, t, h * TOK : (h + 1) * TOK, :] = q * scaled16[h]
            scores[...] = dot_nt(qm[l, t], k)
            for h in range(4):
                rows = slice(h * TOK, (h + 1) * TOK)
                s = scores[rows, :]
                if l == 1:
                    s = jnp.where(same_region, s, MASKED)
                e = jnp.exp(s - jnp.max(s, axis=-1, keepdims=True))
                p = e * (1.0 / jnp.sum(e, axis=-1, keepdims=True))
                probs[l, t, rows, :] = p
                probs16[l, t, rows, :] = p.astype(BF16)
            tmp[...] = dot(probs16[l, t], v)
            att[l, :, 256 * t : 256 * t + 256] = select_heads(tmp).astype(BF16)

    def share_rows(l):
        for i, rows in enumerate((normed_ref, att)):
            both = dot(rows[l], pick).astype(BF16)
            na_own[l, i] = both[:, :256]
            na_out[l, i] = both[:, 256:]
        return to_partner(na_out.at[l], na_in.at[l])

    def backward_values(l, t):
        cols = slice(256 * t, 256 * t + 256)
        g = dot_nt(gy16[l], wo_ref[l, cols, :]).astype(BF16)
        for h in range(4):
            gam[t, h * TOK : (h + 1) * TOK, :] = g * mask16[h]
        gp[l, :, 2 * D + 256 * t : 2 * D + 256 * t + 256] = dot_tn(probs16[l, t], gam[t]).astype(BF16)

    def backward_scores(l, t):
        k = proj[l, :, D + 256 * t : D + 256 * t + 256]
        v = proj[l, :, 2 * D + 256 * t : 2 * D + 256 * t + 256]
        scores[...] = dot_nt(gam[t], v)
        for h in range(4):
            rows = slice(h * TOK, (h + 1) * TOK)
            p = probs[l, t, rows, :]
            g_p = scores[rows, :]
            total = jnp.sum(g_p * p, axis=-1, keepdims=True)
            ds[rows, :] = (p * (g_p - total)).astype(BF16)
        gp[l, :, D + 256 * t : D + 256 * t + 256] = dot_tn(ds[...], qm[l, t]).astype(BF16)
        tmp[...] = dot(ds[...], k)
        gp[l, :, 256 * t : 256 * t + 256] = (select_heads(tmp) * 0.125).astype(BF16)

    def backward_input(l):
        grad_normed = dot_nt(gp[l], wq_ref[l])
        standard = std[l]
        gain_rows = jnp.sum(grad_normed * standard, axis=0, keepdims=True)
        for j in range(4):
            gain_c[0, l * 4 + j : l * 4 + j + 1, :] = gain_rows[:, j * 128 : (j + 1) * 128]
        scaled = grad_normed * gains_ref[l : l + 1, :]
        m1 = jnp.mean(scaled, axis=-1, keepdims=True)
        m2 = jnp.mean(scaled * standard, axis=-1, keepdims=True)
        return gy[l] + inv[l] * (scaled - m1 - standard * m2)

    def send_gp(l, cols):
        return to_partner(gp.at[l, :, cols], gp_in.at[l, :, cols])

    def weight_grad(l, c, first, i, mine, theirs):
        g = dot_tn(na_own[l, i], mine) + dot_tn(na_in[l, i], theirs)
        for j in range(4):
            part = g[:, j * 128 : (j + 1) * 128].astype(BF16)
            gsend[l, c, :, :, first + j] = part.reshape(n_y, 2, 32, 128)

    def value_out_grads(l):
        weight_grad(l, 0, 4, 1, gy16[l], gy_in[l])
        weight_grad(l, 0, 0, 0, gp[l, :, 2 * D :], gp_in[l, :, 2 * D :])

    def query_key_own(l):
        part_g[...] = dot_tn(na_own[l, 0], gp[l, :, : 2 * D])

    def query_key_grads(l):
        g = part_g[...] + dot_tn(na_in[l, 0], gp_in[l, :, : 2 * D])
        for j in range(8):
            part = g[:, j * 128 : (j + 1) * 128].astype(BF16)
            gsend[l, 1, :, :, j] = part.reshape(n_y, 2, 32, 128)

    def stage1(l, c):
        over_y, over_x = [], []
        for k in far_first(4):
            if k < n_y:
                yy = (y + k) % n_y
                over_y.append((gsend.at[l, c, yy, :, 0:4], r1a.at[l, c, k - 1], at_y(yy)))
            xx = (x + k) % 4
            src = gsend.at[l, c, :, xx // 2, pl.ds(4 + 2 * (xx % 2), 2)]
            over_x.append((src, r1b.at[l, c, k - 1], at_x(xx)))
        return remote(r1a.at[l, c], over_y), remote(r1b.at[l, c], over_x)

    def stage2(l, c, copies):
        copies[0].wait_recv()
        for i in range(2):
            total = gsend[l, c, y, i, 0:4].astype(F32)
            for k in range(n_y - 1):
                total = total + r1a[l, c, k, i].astype(F32)
            acca[l, c, i] = total.astype(BF16)
        over_x = []
        for k in far_first(4):
            xx = (x + k) % 4
            src = acca.at[l, c, xx // 2, pl.ds(2 * (xx % 2), 2)]
            over_x.append((src, r2a.at[l, c, k - 1], at_x(xx)))
        over_x = remote(r2a.at[l, c], over_x)
        copies[1].wait_recv()
        for i in range(n_y):
            total = gsend[l, c, i, xhi, pl.ds(4 + 2 * xlo, 2)].astype(F32)
            for k in range(3):
                total = total + r1b[l, c, k, i].astype(F32)
            accb[l, c, i] = total.astype(BF16)
        over_y = []
        for k in far_first(n_y):
            yy = (y + k) % n_y
            over_y.append((accb.at[l, c, yy], r2b.at[l, c, k - 1], at_y(yy)))
        return over_x, remote(r2b.at[l, c], over_y)

    def stage3_sum(l, c, copies):
        for copy in copies:
            copy.wait_recv()
        total = acca[l, c, xhi, pl.ds(2 * xlo, 2)].astype(F32)
        for k in range(3):
            total = total + r2a[l, c, k].astype(F32)
        acc2[l, c, 0:2] = total.reshape(2, 2, 16, 128).astype(BF16)
        total = accb[l, c, y].astype(F32)
        for k in range(n_y - 1):
            total = total + r2b[l, c, k].astype(F32)
        acc2[l, c, 2:4] = total.reshape(2, 2, 16, 128).astype(BF16)

    def stage3(l):
        over_z = []
        for k in far_first(n_z):
            zz = (z + k) % n_z
            over_z.append((acc2.at[l, :, zz // 2, zz % 2], r3.at[l, k - 1], at_z(zz)))
        return remote(r3.at[l], over_z)

    def stage4(l, copies):
        copies.wait_recv()
        total = acc2[l, :, z // 2, z % 2].astype(F32)
        for k in range(n_z - 1):
            total = total + r3[l, k].astype(F32)
        own4[l] = total.astype(BF16)
        over_lat = []
        for k in sorted(range(1, n_lat), key=lambda k: -min(k % n_z, n_z - k % n_z)):
            over_lat.append((own4.at[l], r4.at[l, k - 1], at((a + k) % n_lat, b)))
        return remote(r4.at[l], over_lat)

    def finish(l, copies):
        fin_ref[l, xlo, :, z // 2, z % 2] = own4[l]
        copies.wait_recv()
        for k in range(1, n_lat):
            source = (a + n_lat - k) % n_lat
            zz = source % n_z
            fin_ref[l, source // n_z, :, zz // 2, zz % 2] = r4[l, k - 1]

    def halo_send(step, field_ref, devices):
        copies = []
        for q in range(3):
            hs[step, q] = field_ref[q * QUAD : q * QUAD + PADQ, :].astype(BF16)
            copies.append((hs.at[step, q], hr.at[step, q], devices[q]))
        return remote(hr.at[step], copies)

    def halo_take(step, copies, field_ref):
        copies.wait_recv()
        for q in range(3):
            field_ref[q * QUAD : (q + 1) * QUAD, :] = hr[step, q].astype(F32)[:QUAD]

    loads[0].wait()
    for row, col, start in slab_pieces():
        cols = slice(col, col + WLON // 2)
        xs[0, start : start + WLON, :] = x_ref[row, cols].astype(F32).reshape(WLON, D)
    loads[1].wait()
    last = a == n_lat - 1
    i_id = lax.broadcasted_iota(jnp.int32, (TOK, TOK), 0)
    j_id = lax.broadcasted_iota(jnp.int32, (TOK, TOK), 1)
    cut = jnp.where(last, TOK // 2, TOK)
    same_region = ((i_id < cut) & (j_id < cut)) | ((i_id >= cut) & (j_id >= cut))

    forward(0)
    loads[3].wait()
    middle = xs[0] + dot(att[0], wo_ref[0])
    xs[1] = middle.astype(BF16).astype(F32)
    pl.semaphore_wait(barrier, len(greet))
    mid_copies = halo_send(1, xs.at[1], halo_down)
    loads[4].wait()
    for row, col, start in slab_pieces():
        cols = slice(col, col + WLON // 2)
        gy[1, start : start + WLON, :] = c_ref[row, cols].astype(F32).reshape(WLON, D)
    cot_copies = halo_send(0, gy.at[1], halo_down)
    na_copies = [share_rows(0)]

    halo_take(1, mid_copies, xs.at[1])
    forward(1)
    halo_take(0, cot_copies, gy.at[1])
    gy16[1] = gy[1].astype(BF16)
    gy_copies = [to_partner(gy16.at[1], gy_in.at[1])]
    loads[6].wait()
    backward_values(1, 0)
    backward_values(1, 1)
    v_copies = [send_gp(1, slice(2 * D, 3 * D))]
    backward_scores(1, 0)
    backward_scores(1, 1)
    qk_copies = [send_gp(1, slice(0, 2 * D))]
    xs[1] = backward_input(1).astype(BF16).astype(F32)
    back_copies = halo_send(2, xs.at[1], halo_up)
    gy[0, 3 * QUAD :, :] = xs[1, 3 * QUAD :, :]
    na_copies.append(share_rows(1))
    na_copies[1].wait_recv()
    gy_copies[0].wait_recv()
    v_copies[0].wait_recv()
    value_out_grads(1)
    s1v = stage1(1, 0)
    query_key_own(1)
    qk_copies[0].wait_recv()
    query_key_grads(1)
    s1q = stage1(1, 1)

    halo_take(2, back_copies, gy.at[0])
    gy16[0] = gy[0].astype(BF16)
    gy_copies.append(to_partner(gy16.at[0], gy_in.at[0]))
    backward_values(0, 0)
    backward_values(0, 1)
    v_copies.append(send_gp(0, slice(2 * D, 3 * D)))
    backward_scores(0, 0)
    na_copies[0].wait_recv()
    gy_copies[1].wait_recv()
    v_copies[1].wait_recv()
    value_out_grads(0)
    t1v = stage1(0, 0)
    backward_scores(0, 1)
    qk_copies.append(send_gp(0, slice(0, 2 * D)))
    s2v = stage2(1, 0, s1v)
    query_key_own(0)
    qk_copies[1].wait_recv()
    query_key_grads(0)
    t1q = stage1(0, 1)
    s2q = stage2(1, 1, s1q)
    xs[0] = backward_input(0)
    for row, col, start in slab_pieces():
        piece = xs[0, start : start + WLON, :].reshape(WLON // 2, LEV, D)
        gx_ref[row, col : col + WLON // 2] = piece.astype(BF16)
    stores = [local(7, gx_ref, gx_hbm)]

    def gain_send(buf, peers):
        return remote(
            buf.at[pl.ds(1, len(peers))],
            [(buf.at[0], buf.at[k + 1], device) for k, device in enumerate(peers)],
        )

    def gain_sum(buf, copies, me, n):
        copies.wait_recv()
        total = buf[me]
        for j in range(1, n):
            total = total + buf[(me + n - j) % n]
        return total

    g1 = gain_send(gain_c, [partner])
    t2v = stage2(0, 0, t1v)
    stage3_sum(1, 0, s2v)
    stage3_sum(1, 1, s2q)
    s3 = stage3(1)
    gain_y[0] = gain_sum(gain_c, g1, core, 2)
    g2 = gain_send(gain_y, [at_y((y + k) % n_y) for k in range(1, n_y)])
    t2q = stage2(0, 1, t1q)
    gain_x[0] = gain_sum(gain_y, g2, y, n_y)
    g3 = gain_send(gain_x, [at_x((x + k) % 4) for k in range(1, 4)])
    stage3_sum(0, 0, t2v)
    stage3_sum(0, 1, t2q)
    t3 = stage3(0)
    s4 = stage4(1, s3)
    gain_z[0] = gain_sum(gain_x, g3, x, 4)
    g4 = gain_send(gain_z, [at_z((z + k) % n_z) for k in range(1, n_z)])
    t4 = stage4(0, t3)
    total = gain_sum(gain_z, g4, z, n_z)
    for l in range(2):
        for j in range(4):
            gg_ref[l : l + 1, j * 128 : (j + 1) * 128] = total[l * 4 + j : l * 4 + j + 1, :]
    finish(1, s4)
    finish(0, t4)
    stores[0].wait()
    for copy in pending:
        copy.wait_send()


def unpack(gx_ref, fin_ref, gg_ref, gx_out, gq_out, go_out, gg_out):
    gx_out[...] = gx_ref[...]
    gg_out[...] = gg_ref[...]
    for l in range(2):
        for lo in range(2):
            for j in range(2):
                cols = slice((2 * lo + j) * 128, (2 * lo + j + 1) * 128)
                block = [
                    [fin_ref[l, lo, c, 2 * h + j].reshape(32, 128).astype(F32) for h in range(2)]
                    for c in range(2)
                ]
                gq_out[l, :, cols] = block[1][0]
                gq_out[l, :, D + cols.start : D + cols.stop] = block[1][1]
                gq_out[l, :, 2 * D + cols.start : 2 * D + cols.stop] = block[0][0]
                go_out[l, :, cols] = block[0][1]


N_GROUPS = 35


def shards(n_lat, n_lon, inputs, cotangent, gains, w_qkv, w_out):
    n_y, n_z = n_lon // 4, n_lat // 2
    vmem = pl.BlockSpec(memory_space=pltpu.VMEM)
    hbm = pl.BlockSpec(memory_space=pl.ANY)
    scratch = [
        pltpu.VMEM((WLAT, WLON, LEV, D), BF16),
        pltpu.VMEM((WLAT, WLON, LEV, D), BF16),
        pltpu.VMEM((2, D), F32),
        pltpu.VMEM((2, D, 3 * D), BF16),
        pltpu.VMEM((2, D, D), BF16),
        pltpu.VMEM((WLAT, WLON, LEV, D), BF16),
        pltpu.VMEM((2, TOK, D), F32),
        pltpu.VMEM((2, TOK, D), F32),
        pltpu.VMEM((2, TOK, D), F32),
        pltpu.VMEM((2, TOK, 1), F32),
        pltpu.VMEM((2, TOK, 3 * D), BF16),
        pltpu.VMEM((2, 2, STACK, 256), BF16),
        pltpu.VMEM((2, STACK, 256), BF16),
        pltpu.VMEM((2, 2, STACK, TOK), F32),
        pltpu.VMEM((2, 2, STACK, TOK), BF16),
        pltpu.VMEM((2, TOK, D), BF16),
        pltpu.VMEM((STACK, 256), F32),
        pltpu.VMEM((STACK, TOK), F32),
        pltpu.VMEM((STACK, TOK), BF16),
        pltpu.VMEM((2, TOK, 3 * D), BF16),
        pltpu.VMEM((2, TOK, D), BF16),
        pltpu.VMEM((2, 2, TOK, 256), BF16),
        pltpu.VMEM((2, 2, TOK, 256), BF16),
        pltpu.VMEM((2, 2, TOK, 256), BF16),
        pltpu.VMEM((2, TOK, 3 * D), BF16),
        pltpu.VMEM((2, TOK, D), BF16),
        pltpu.VMEM((3, 3, PADQ, D), BF16),
        pltpu.VMEM((3, 3, PADQ, D), BF16),
        pltpu.VMEM((2, 2, n_y, 2, 8, 32, 128), BF16),
        pltpu.VMEM((2, 2, n_y - 1, 2, 4, 32, 128), BF16),
        pltpu.VMEM((2, 2, 3, n_y, 2, 32, 128), BF16),
        pltpu.VMEM((2, 2, 2, 4, 32, 128), BF16),
        pltpu.VMEM((2, 2, n_y, 2, 32, 128), BF16),
        pltpu.VMEM((2, 2, 3, 2, 32, 128), BF16),
        pltpu.VMEM((2, 2, n_y - 1, 2, 32, 128), BF16),
        pltpu.VMEM((2, 2, 4, 2, 16, 128), BF16),
        pltpu.VMEM((2, n_z - 1, 2, 16, 128), BF16),
        pltpu.VMEM((2, 2, 16, 128), BF16),
        pltpu.VMEM((2, n_lat - 1, 2, 16, 128), BF16),
        pltpu.VMEM((2, TOK, D), BF16),
        pltpu.VMEM((D // 2, 2 * D), F32),
        pltpu.VMEM((2, 8, 128), F32),
        pltpu.VMEM((n_y, 8, 128), F32),
        pltpu.VMEM((4, 8, 128), F32),
        pltpu.VMEM((n_z, 8, 128), F32),
        pltpu.SemaphoreType.DMA((N_GROUPS,)),
        pltpu.SemaphoreType.DMA((N_GROUPS,)),
        pltpu.SemaphoreType.DMA((8,)),
    ]
    swap = (1, 2, 0, 3)
    gx, fin, gg = pl.pallas_call(
        functools.partial(kernel, n_lat, n_lon),
        out_shape=(
            jax.ShapeDtypeStruct((WLAT, WLON, LEV, D), BF16),
            jax.ShapeDtypeStruct((2, 2, 2, 4, 2, 16, 128), BF16),
            jax.ShapeDtypeStruct((2, D), F32),
        ),
        in_specs=[hbm] * 5,
        out_specs=(hbm, vmem, vmem),
        scratch_shapes=scratch,
        compiler_params=pltpu.CompilerParams(
            collective_id=0, has_side_effects=True, vmem_limit_bytes=56 * 2**20
        ),
    )(inputs.transpose(swap), cotangent.transpose(swap), gains, w_qkv, w_out)
    gx, gq, go, gg = pl.pallas_call(
        unpack,
        out_shape=(
            jax.ShapeDtypeStruct(gx.shape, BF16),
            jax.ShapeDtypeStruct((2, D // n_lon, 3 * D), F32),
            jax.ShapeDtypeStruct((2, D // n_lon, D), F32),
            jax.ShapeDtypeStruct((2, D), F32),
        ),
        in_specs=[vmem] * 3,
        out_specs=(vmem,) * 4,
    )(gx, fin, gg)
    return gx.transpose(2, 0, 1, 3), gq, go, gg


def solution(mesh):
    in_specs = (P(None, "lat", "lon", None), P(None, "lat", "lon", None), P(), P(), P())
    out_specs = (P(None, "lat", "lon", None), P(None, "lon", None), P(None, "lon", None), P())
    return jax.shard_map(
        functools.partial(shards, mesh.shape["lat"], mesh.shape["lon"]),
        mesh=mesh,
        in_specs=in_specs,
        out_specs=out_specs,
        check_vma=False,
    )
```
